256 devices in a mesh: vir: 16 (over x, z_lo, core), occ: 16 (over z_hi, y).
Axes of the slice: x: 4, y: 4, z: 8 (z_hi: 4, z_lo: 2; z = z_hi * 2 + z_lo), core: 2. Of those that a mesh axis runs over, the one named last changes fastest.
Arguments:
- amplitudes: bfloat16 [16384, 8192], P('occ'), may hold values from -6 to 6
- integrals: bfloat16 [8192, 8192], P('occ', 'vir'), may hold values from -0.1875 to 0.1875
- tile_irrep: int32 [64], replicated, may hold values from 0 to 3
- tile_spin: int32 [64], replicated, may hold values from 0 to 1
- row_mirror: int32 [16384], P('occ'), may hold values from 0 to 16383, as said below
- col_mirror: int32 [8192], P('vir'), may hold values from 0 to 8191, as said below
- occ_gap: float32 [16384], P('occ'), may hold values from 0.5 to 2
- vir_energy: float32 [8192], P('vir'), may hold values from 0.5 to 4
Outputs:
- new_amps: float32 [16384, 8192], P('occ', 'vir')
The draws below stay inside these ranges and needn't reach their ends.
Inputs may be any that keep to these rules, and one draw needn't show every extreme that they name: row_mirror is an involution with no fixed point; a row of occupied block k (blocks of 1024 rows in order) has its mirror in block (k + 8) modulo 16. col_mirror is an involution with no fixed point; a pair of virtual block k (blocks of 512 pairs in order) has its mirror in block (k + 8) modulo 16.
All inputs are finite; a program needn't handle non-finite values.
Results may differ from the reference program's by a relative error of at most 0.0003.
Values may be sent and summed in bfloat16 or wider, within the bound.
A program may use at most 128 MiB of HBM per device.

```python
import math
import jax
import jax.numpy as jnp

TILE = 128
TILES = 64
OP_DEV = 1024
IRREPS = 4
SPINS = 2
PAIRS = 8192
PAIR_DEV = 512
OP = 16384


def mirror_table(key, total, block):
    halves = total // block // 2
    keys = jax.random.split(key, halves)
    forward = jax.vmap(lambda one_key: jax.random.permutation(one_key, block))(keys).astype(jnp.int32)
    backward = jnp.argsort(forward, axis=1, stable=True).astype(jnp.int32)
    base = jnp.arange(halves, dtype=jnp.int32)[:, None] * block
    lower = base + halves * block + forward
    upper = base + backward
    return jnp.concatenate([lower, upper], axis=0).reshape(total)


def draw_row_mirror(key, part):
    key = jax.random.fold_in(key, 11)
    return mirror_table(key, OP, OP_DEV)


def draw_col_mirror(key, part):
    key = jax.random.fold_in(key, 12)
    return mirror_table(key, PAIRS, PAIR_DEV)


def touch_ends(entries, rng, low, top_value):
    longest = entries.shape.index(max(entries.shape))
    spots = []
    for shift in (0, 1):
        where = [jax.random.randint(jax.random.fold_in(rng, axis), (), 0, length) for axis, length in enumerate(entries.shape)]
        where[longest] = (where[longest] + shift) % entries.shape[longest]
        spots.append(tuple(where))
    return entries.at[spots[0]].set(low).at[spots[1]].set(top_value)


def block_scale(key, shape, shards, smallest, top_value):
    def one(dim, parts):
        steps = jax.random.uniform(jax.random.fold_in(jax.random.fold_in(key, 6), dim), (parts,), jnp.float32, smallest / len(shards), top_value / len(shards))
        return jnp.repeat(jnp.exp(steps), shape[dim] // parts).reshape((-1,) + (1,) * (len(shape) - dim - 1))

    level = one(*shards[0])
    for cut in shards[1:]:
        level = level * one(*cut)
    return level


def normal_values(rng, dims, scale, reach, pieces=(), kind=jnp.bfloat16):
    loudness = block_scale(rng, dims, pieces, -0.22, 0.18) if pieces else 1.0
    values = jax.random.normal(rng, dims, jnp.float32) * scale * loudness
    return jnp.minimum(jnp.maximum(values, -reach), reach).astype(kind)


def setup_inputs(seed: int = 0) -> dict:
    key_of = jax.random.split(jax.random.key(seed), 9)
    return {
        "amplitudes": normal_values(key_of[0], (OP, PAIRS), 1.0, 6.0, ((0, 16),)),
        "integrals": normal_values(key_of[1], (PAIRS, PAIRS), (PAIRS // (IRREPS * SPINS)) ** -0.5, 0.1875, ((0, 16), (1, 16))),
        "tile_irrep": touch_ends(jax.random.randint(key_of[2], (TILES,), 0, IRREPS), jax.random.fold_in(key_of[2], 1), 0, IRREPS - 1).astype(jnp.int32),
        "tile_spin": touch_ends(jax.random.randint(key_of[3], (TILES,), 0, SPINS), jax.random.fold_in(key_of[3], 1), 0, SPINS - 1).astype(jnp.int32),
        "row_mirror": draw_row_mirror(jax.random.fold_in(key_of[8], 71), 0),
        "col_mirror": draw_col_mirror(jax.random.fold_in(key_of[8], 71), 0),
        "occ_gap": jnp.clip(jnp.exp(math.log(2.0) - 1.3862944 * jax.random.uniform(key_of[6], (OP,), jnp.float32) ** block_scale(key_of[6], (OP,), ((0, 16),), -0.2, 0.2)), 0.5, 2.0),
        "vir_energy": jnp.clip(jnp.exp(math.log(4.0) - 2.0794415 * jax.random.uniform(key_of[7], (PAIRS,), jnp.float32) ** block_scale(key_of[7], (PAIRS,), ((0, 16),), -0.2, 0.2)), 0.5, 4.0),
    }


def reference(amplitudes, integrals, tile_irrep, tile_spin, row_mirror, col_mirror, occ_gap, vir_energy):
    code = tile_irrep * SPINS + tile_spin
    pair_codes = jnp.repeat(code, TILE)
    masked = jnp.where(pair_codes[:, None] == pair_codes[None, :], integrals, jnp.zeros((), jnp.bfloat16))
    ladder = jnp.dot(amplitudes, masked, preferred_element_type=jnp.float32)
    rows_anti = ladder - jnp.take(ladder, row_mirror, axis=0)
    residual = rows_anti - jnp.take(rows_anti, col_mirror, axis=1)
    return residual / (occ_gap[:, None] + vir_energy[None, :])
```

```python
import functools
import jax
import jax.numpy as jnp
from jax import lax
from jax.sharding import PartitionSpec as P
from jax.experimental import pallas as pl
from jax.experimental.pallas import tpu as pltpu

TILE = 128
SPINS = 2
MESH = pl.DeviceIdType.MESH
CHUNK = 128
LEVELS = 32767.0
TINY = 1e-30
VMEM = pl.BlockSpec(memory_space=pltpu.VMEM)


def permuted(one_hot, x):
    hi = x.astype(jnp.bfloat16)
    lo = (x - hi.astype(jnp.float32)).astype(jnp.bfloat16)
    dot = functools.partial(jnp.dot, preferred_element_type=jnp.float32)
    return dot(one_hot, hi) + dot(one_hot, lo)


def permuted_cols(x, one_hot, transposed):
    hi = x.astype(jnp.bfloat16)
    lo = (x - hi.astype(jnp.float32)).astype(jnp.bfloat16)
    dims = (((1,), (1 if transposed else 0,)), ((), ()))
    dot = functools.partial(lax.dot_general, dimension_numbers=dims, preferred_element_type=jnp.float32)
    return dot(hi, one_hot) + dot(lo, one_hot)


def coded(x, top):
    return jnp.round(x * (LEVELS / top)).astype(jnp.int32).astype(jnp.int16)


def decoded(code, top):
    return code.astype(jnp.int32).astype(jnp.float32) * (top / LEVELS)


def exchange_kernel(
    ladder, row_here, row_there, col_there, out,
    own, sent_first, out_x1, in_x1, out_z, in_z, out_x2, in_x2, tops_out, tops_in, diff, to_rows, from_rows, cols,
    sends, recvs, top_sends, top_recvs,
):
    vir, occ = lax.axis_index("vir"), lax.axis_index("occ")
    virs, occs = lax.axis_size("vir"), lax.axis_size("occ")
    x_peer = (lax.rem(vir + virs // 2, virs), occ)
    z_peer = (vir, lax.rem(occ + occs // 2, occs))
    rows, width = ladder.shape
    half = width // 2
    chunks = rows // CHUNK
    lower = vir < virs // 2
    sign = jnp.where(lower, 1.0, -1.0).astype(jnp.float32)
    kept = pl.multiple_of(jnp.where(lower, 0, half), half)
    given = pl.multiple_of(half - kept, half)

    barrier = pltpu.get_barrier_semaphore()
    for peer in (x_peer, z_peer):
        pl.semaphore_signal(barrier, inc=1, device_id=peer, device_id_type=MESH)

    cols[...] = (
        lax.broadcasted_iota(jnp.int32, (width, width), 0)
        == jnp.where(lower, lax.broadcasted_iota(jnp.int32, (1, width), 1), col_there[...])
    ).astype(jnp.float32).astype(jnp.bfloat16)

    def make_to(c, _):
        at = pl.ds(pl.multiple_of(c * CHUNK, CHUNK), CHUNK)
        to_rows[at, :] = (
            lax.broadcasted_iota(jnp.int32, (CHUNK, rows), 0) + c * CHUNK == row_there[...]
        ).astype(jnp.float32).astype(jnp.bfloat16)
        return 0

    def make_from(c, _):
        at = pl.ds(pl.multiple_of(c * CHUNK, CHUNK), CHUNK)
        from_rows[at, :] = (
            lax.broadcasted_iota(jnp.int32, (CHUNK, rows), 1) == row_here[at, :][:, :1]
        ).astype(jnp.float32).astype(jnp.bfloat16)
        return 0

    lax.fori_loop(0, chunks, make_to, 0)

    def order_cols(c, _):
        at = pl.ds(pl.multiple_of(c * CHUNK, CHUNK), CHUNK)
        own[at, :] = permuted_cols(ladder[at, :], cols[...], True)
        return 0

    lax.fori_loop(0, chunks, order_cols, 0)

    def order_rows(c, _):
        at = pl.ds(pl.multiple_of(c * CHUNK, CHUNK), CHUNK)
        moved = permuted(to_rows[at, :], own[...])
        sent_first[at, :] = moved
        top = jnp.maximum(jnp.max(jnp.abs(moved), axis=0, keepdims=True), TINY)
        diff_top = top
        tops_out[0, pl.ds(c, 1), :] = diff_top[:, :half]
        tops_out[1, pl.ds(c, 1), :] = diff_top[:, half:]
        return 0

    lax.fori_loop(0, chunks, order_rows, 0)
    pl.semaphore_wait(barrier, 2)

    def tops(slot, source, peer):
        return pltpu.make_async_remote_copy(
            source, tops_in.at[slot], top_sends.at[slot], top_recvs.at[slot], device_id=peer, device_id_type=MESH
        )

    def piece(phase, c, source, target, peer):
        at = pl.ds(pl.multiple_of(c * CHUNK, CHUNK), CHUNK)
        return pltpu.make_async_remote_copy(
            source.at[at], target.at[at], sends.at[phase, c], recvs.at[phase, c], device_id=peer, device_id_type=MESH
        )

    keep_slot = jnp.where(lower, 0, 1)
    tops_out[2, :, :] = tops_out[1 - keep_slot, :, :]
    first_tops = tops(0, tops_out.at[2], x_peer)
    first_tops.start()

    def send_first(c, _):
        at = pl.ds(pl.multiple_of(c * CHUNK, CHUNK), CHUNK)
        out_x1[at, :] = coded(sent_first[at, pl.ds(given, half)], tops_out[2, pl.ds(c, 1), :])
        piece(0, c, out_x1, in_x1, x_peer).start()
        return 0

    lax.fori_loop(0, chunks, send_first, 0)
    lax.fori_loop(0, chunks, make_from, 0)

    first_tops.wait()
    tops_out[3, :, :] = tops_out[keep_slot, :, :] + tops_in[0, :, :]
    second_tops = tops(1, tops_out.at[3], z_peer)
    second_tops.start()

    def send_second(c, _):
        at = pl.ds(pl.multiple_of(c * CHUNK, CHUNK), CHUNK)
        piece(0, c, out_x1, in_x1, x_peer).wait()
        came = decoded(in_x1[at, :], tops_in[0, pl.ds(c, 1), :])
        diff[at, :] = came
        out_z[at, :] = coded(sign * (sent_first[at, pl.ds(kept, half)] - came), tops_out[3, pl.ds(c, 1), :])
        piece(1, c, out_z, in_z, z_peer).start()
        return 0

    lax.fori_loop(0, chunks, send_second, 0)
    second_tops.wait()

    def back(c, _):
        at = pl.ds(pl.multiple_of(c * CHUNK, CHUNK), CHUNK)
        mine = sign * (own[at, pl.ds(kept, half)] - permuted(from_rows[at, :], diff[...]))
        own[at, pl.ds(kept, half)] = mine
        tops_out[4, pl.ds(c, 1), :] = jnp.max(jnp.abs(mine), axis=0, keepdims=True) + tops_in[1, pl.ds(c, 1), :]
        return 0

    lax.fori_loop(0, chunks, back, 0)
    third_tops = tops(2, tops_out.at[4], x_peer)
    third_tops.start()

    def send_third(c, _):
        at = pl.ds(pl.multiple_of(c * CHUNK, CHUNK), CHUNK)
        piece(1, c, out_z, in_z, z_peer).wait()
        done = own[at, pl.ds(kept, half)] - decoded(in_z[at, :], tops_in[1, pl.ds(c, 1), :])
        own[at, pl.ds(kept, half)] = done
        out_x2[at, :] = coded(done, tops_out[4, pl.ds(c, 1), :])
        piece(2, c, out_x2, in_x2, x_peer).start()
        return 0

    lax.fori_loop(0, chunks, send_third, 0)
    third_tops.wait()

    def finish(c, _):
        at = pl.ds(pl.multiple_of(c * CHUNK, CHUNK), CHUNK)
        piece(2, c, out_x2, in_x2, x_peer).wait()
        own[at, pl.ds(given, half)] = decoded(in_x2[at, :], tops_in[2, pl.ds(c, 1), :])
        out[at, :] = sign * permuted_cols(own[at, :], cols[...], False)
        return 0

    lax.fori_loop(0, chunks, finish, 0)


def exchanged(ladder, row_local, col_local):
    rows, width = ladder.shape
    half = width // 2
    chunks = rows // CHUNK
    f32, i16, bf16 = jnp.float32, jnp.int16, jnp.bfloat16
    return pl.pallas_call(
        exchange_kernel,
        out_shape=jax.ShapeDtypeStruct((rows, width), f32),
        in_specs=[VMEM] * 4,
        out_specs=VMEM,
        scratch_shapes=[
            pltpu.VMEM((rows, width), f32),
            pltpu.VMEM((rows, width), f32),
        ]
        + [pltpu.VMEM((rows, half), i16)] * 6
        + [
            pltpu.VMEM((5, chunks, half), f32),
            pltpu.VMEM((3, chunks, half), f32),
            pltpu.VMEM((rows, half), f32),
            pltpu.VMEM((rows, rows), bf16),
            pltpu.VMEM((rows, rows), bf16),
            pltpu.VMEM((width, width), bf16),
            pltpu.SemaphoreType.DMA((3, chunks)),
            pltpu.SemaphoreType.DMA((3, chunks)),
            pltpu.SemaphoreType.DMA((3,)),
            pltpu.SemaphoreType.DMA((3,)),
        ],
        compiler_params=pltpu.CompilerParams(collective_id=1, has_side_effects=True, vmem_limit_bytes=48 << 20),
        name="exchange",
    )(ladder, jnp.broadcast_to(row_local[:, None], (rows, TILE)), row_local[None, :], col_local[None, :])


def local(amplitudes, integrals, tile_irrep, tile_spin, row_mirror, col_mirror, occ_gap, vir_energy):
    row_count, col_count = integrals.shape
    row_tiles = row_count // TILE
    col_tiles = col_count // TILE
    code = tile_irrep * SPINS + tile_spin
    row_codes = lax.dynamic_slice_in_dim(code, lax.axis_index("occ") * row_tiles, row_tiles)
    col_codes = lax.dynamic_slice_in_dim(code, lax.axis_index("vir") * col_tiles, col_tiles)
    allowed = row_codes[:, None] == col_codes[None, :]
    masked = jnp.where(
        allowed[:, None, :, None], integrals.reshape(row_tiles, TILE, col_tiles, TILE), 0
    ).reshape(row_count, col_count)
    row_local = jnp.remainder(row_mirror, amplitudes.shape[0])
    col_local = jnp.remainder(col_mirror, col_count)
    ladder = jnp.dot(
        amplitudes, lax.all_gather(masked, "occ", axis=0, tiled=True), preferred_element_type=jnp.float32
    )
    residual = exchanged(ladder, row_local, col_local)
    return residual / (occ_gap[:, None] + vir_energy[None, :])


def solution(mesh):
    placed = (P("occ", None), P("occ", "vir"), P(), P(), P("occ"), P("vir"), P("occ"), P("vir"))
    return jax.shard_map(
        local, mesh=mesh, in_specs=placed, out_specs=P("occ", "vir"), check_vma=False
    )
```

```python
import functools
import jax
import jax.numpy as jnp
from jax import lax
from jax.sharding import PartitionSpec as P
from jax.experimental import pallas as pl
from jax.experimental.pallas import tpu as pltpu

TILE = 128
SPINS = 2
MESH = pl.DeviceIdType.MESH
CHUNK = 128
LEVELS = 32767.0
TINY = 1e-30
VMEM = pl.BlockSpec(memory_space=pltpu.VMEM)


def permuted(one_hot, x):
    hi = x.astype(jnp.bfloat16)
    lo = (x - hi.astype(jnp.float32)).astype(jnp.bfloat16)
    dot = functools.partial(jnp.dot, preferred_element_type=jnp.float32)
    return dot(one_hot, hi) + dot(one_hot, lo)


def permuted_cols(x, one_hot, transposed):
    hi = x.astype(jnp.bfloat16)
    lo = (x - hi.astype(jnp.float32)).astype(jnp.bfloat16)
    dims = (((1,), (1 if transposed else 0,)), ((), ()))
    dot = functools.partial(lax.dot_general, dimension_numbers=dims, preferred_element_type=jnp.float32)
    return dot(hi, one_hot) + dot(lo, one_hot)


def coded(x, top):
    return jnp.round(x * (LEVELS / top)).astype(jnp.int32).astype(jnp.int16)


def decoded(code, top):
    return code.astype(jnp.int32).astype(jnp.float32) * (top / LEVELS)


def exchange_kernel(
    ladder, row_here, row_there, col_there, out,
    own, sent_first, out_x1, in_x1, out_z, in_z, out_x2, in_x2, tops_out, tops_in, diff, to_rows, from_rows, cols,
    sends, recvs, top_sends, top_recvs,
):
    vir, occ = lax.axis_index("vir"), lax.axis_index("occ")
    virs, occs = lax.axis_size("vir"), lax.axis_size("occ")
    x_peer = (lax.rem(vir + virs // 2, virs), occ)
    z_peer = (vir, lax.rem(occ + occs // 2, occs))
    rows, width = ladder.shape
    half = width // 2
    chunks = rows // CHUNK
    lower = vir < virs // 2
    sign = jnp.where(lower, 1.0, -1.0).astype(jnp.float32)
    kept = pl.multiple_of(jnp.where(lower, 0, half), half)
    given = pl.multiple_of(half - kept, half)

    barrier = pltpu.get_barrier_semaphore()
    for peer in (x_peer, z_peer):
        pl.semaphore_signal(barrier, inc=1, device_id=peer, device_id_type=MESH)

    cols[...] = (
        lax.broadcasted_iota(jnp.int32, (width, width), 0)
        == jnp.where(lower, lax.broadcasted_iota(jnp.int32, (1, width), 1), col_there[...])
    ).astype(jnp.float32).astype(jnp.bfloat16)

    def make_to(c, _):
        at = pl.ds(pl.multiple_of(c * CHUNK, CHUNK), CHUNK)
        to_rows[at, :] = (
            lax.broadcasted_iota(jnp.int32, (CHUNK, rows), 0) + c * CHUNK == row_there[...]
        ).astype(jnp.float32).astype(jnp.bfloat16)
        return 0

    def make_from(c, _):
        at = pl.ds(pl.multiple_of(c * CHUNK, CHUNK), CHUNK)
        from_rows[at, :] = (
            lax.broadcasted_iota(jnp.int32, (CHUNK, rows), 1) == row_here[at, :][:, :1]
        ).astype(jnp.float32).astype(jnp.bfloat16)
        return 0

    lax.fori_loop(0, chunks, make_to, 0)

    def order_cols(c, _):
        at = pl.ds(pl.multiple_of(c * CHUNK, CHUNK), CHUNK)
        own[at, :] = permuted_cols(ladder[at, :], cols[...], True)
        return 0

    lax.fori_loop(0, chunks, order_cols, 0)

    def order_rows(c, _):
        at = pl.ds(pl.multiple_of(c * CHUNK, CHUNK), CHUNK)
        moved = permuted(to_rows[at, :], own[...])
        sent_first[at, :] = moved
        top = jnp.maximum(jnp.max(jnp.abs(moved), axis=0, keepdims=True), TINY)
        diff_top = top
        tops_out[0, pl.ds(c, 1), :] = diff_top[:, :half]
        tops_out[1, pl.ds(c, 1), :] = diff_top[:, half:]
        return 0

    lax.fori_loop(0, chunks, order_rows, 0)
    pl.semaphore_wait(barrier, 2)

    def tops(slot, source, peer):
        return pltpu.make_async_remote_copy(
            source, tops_in.at[slot], top_sends.at[slot], top_recvs.at[slot], device_id=peer, device_id_type=MESH
        )

    def piece(phase, c, source, target, peer):
        at = pl.ds(pl.multiple_of(c * CHUNK, CHUNK), CHUNK)
        return pltpu.make_async_remote_copy(
            source.at[at], target.at[at], sends.at[phase, c], recvs.at[phase, c], device_id=peer, device_id_type=MESH
        )

    keep_slot = jnp.where(lower, 0, 1)
    tops_out[2, :, :] = tops_out[1 - keep_slot, :, :]
    first_tops = tops(0, tops_out.at[2], x_peer)
    first_tops.start()

    def send_first(c, _):
        at = pl.ds(pl.multiple_of(c * CHUNK, CHUNK), CHUNK)
        out_x1[at, :] = coded(sent_first[at, pl.ds(given, half)], tops_out[2, pl.ds(c, 1), :])
        piece(0, c, out_x1, in_x1, x_peer).start()
        return 0

    lax.fori_loop(0, chunks, send_first, 0)
    lax.fori_loop(0, chunks, make_from, 0)

    first_tops.wait()
    tops_out[3, :, :] = tops_out[keep_slot, :, :] + tops_in[0, :, :]
    second_tops = tops(1, tops_out.at[3], z_peer)
    second_tops.start()

    def send_second(c, _):
        at = pl.ds(pl.multiple_of(c * CHUNK, CHUNK), CHUNK)
        piece(0, c, out_x1, in_x1, x_peer).wait()
        came = decoded(in_x1[at, :], tops_in[0, pl.ds(c, 1), :])
        diff[at, :] = came
        out_z[at, :] = coded(sign * (sent_first[at, pl.ds(kept, half)] - came), tops_out[3, pl.ds(c, 1), :])
        piece(1, c, out_z, in_z, z_peer).start()
        return 0

    lax.fori_loop(0, chunks, send_second, 0)
    second_tops.wait()

    def back(c, _):
        at = pl.ds(pl.multiple_of(c * CHUNK, CHUNK), CHUNK)
        mine = sign * (own[at, pl.ds(kept, half)] - permuted(from_rows[at, :], diff[...]))
        own[at, pl.ds(kept, half)] = mine
        tops_out[4, pl.ds(c, 1), :] = jnp.max(jnp.abs(mine), axis=0, keepdims=True) + tops_in[1, pl.ds(c, 1), :]
        return 0

    lax.fori_loop(0, chunks, back, 0)
    third_tops = tops(2, tops_out.at[4], x_peer)
    third_tops.start()

    def send_third(c, _):
        at = pl.ds(pl.multiple_of(c * CHUNK, CHUNK), CHUNK)
        piece(1, c, out_z, in_z, z_peer).wait()
        done = own[at, pl.ds(kept, half)] - decoded(in_z[at, :], tops_in[1, pl.ds(c, 1), :])
        own[at, pl.ds(kept, half)] = done
        out_x2[at, :] = coded(done, tops_out[4, pl.ds(c, 1), :])
        piece(2, c, out_x2, in_x2, x_peer).start()
        return 0

    lax.fori_loop(0, chunks, send_third, 0)
    third_tops.wait()

    def finish(c, _):
        at = pl.ds(pl.multiple_of(c * CHUNK, CHUNK), CHUNK)
        piece(2, c, out_x2, in_x2, x_peer).wait()
        own[at, pl.ds(given, half)] = decoded(in_x2[at, :], tops_in[2, pl.ds(c, 1), :])
        out[at, :] = sign * permuted_cols(own[at, :], cols[...], False)
        return 0

    lax.fori_loop(0, chunks, finish, 0)


def exchanged(ladder, row_local, col_local):
    rows, width = ladder.shape
    half = width // 2
    chunks = rows // CHUNK
    f32, i16, bf16 = jnp.float32, jnp.int16, jnp.bfloat16
    return pl.pallas_call(
        exchange_kernel,
        out_shape=jax.ShapeDtypeStruct((rows, width), f32),
        in_specs=[VMEM] * 4,
        out_specs=VMEM,
        scratch_shapes=[
            pltpu.VMEM((rows, width), f32),
            pltpu.VMEM((rows, width), f32),
        ]
        + [pltpu.VMEM((rows, half), i16)] * 6
        + [
            pltpu.VMEM((5, chunks, half), f32),
            pltpu.VMEM((3, chunks, half), f32),
            pltpu.VMEM((rows, half), f32),
            pltpu.VMEM((rows, rows), bf16),
            pltpu.VMEM((rows, rows), bf16),
            pltpu.VMEM((width, width), bf16),
            pltpu.SemaphoreType.DMA((3, chunks)),
            pltpu.SemaphoreType.DMA((3, chunks)),
            pltpu.SemaphoreType.DMA((3,)),
            pltpu.SemaphoreType.DMA((3,)),
        ],
        compiler_params=pltpu.CompilerParams(collective_id=1, has_side_effects=True, vmem_limit_bytes=48 << 20),
        name="exchange",
    )(ladder, jnp.broadcast_to(row_local[:, None], (rows, TILE)), row_local[None, :], col_local[None, :])


SLOTS = 40
TERMS = 18
SLICES = 8
FINE = TILE // SLICES
SHARED = 16
ROW_STEP = 256


def ladder_kernel(
    pack_from, term_slot, term_tile, blocks, amplitudes, ladder,
    spread, tiles, amps, factor,
    amp_sems, spread_sends, spread_recvs, z_sends, z_recvs, y_sends, y_recvs, core_sends, core_recvs,
):
    vir, occ = lax.axis_index("vir"), lax.axis_index("occ")
    core, y, z = lax.rem(vir, 2), lax.rem(occ, 4), occ // 4
    pair = vir - core
    me = 2 * y + core
    rows = ladder.shape[0]
    half = SLOTS // 2

    def beside(step):
        to = lax.rem(me + step, SLICES)
        return to, (pair + lax.rem(to, 2), z * 4 + to // 2)

    def along_z(step):
        return (vir, lax.rem(z + step, 4) * 4 + y)

    def along_y(step):
        return (vir, z * 4 + lax.rem(y + step, 4))

    mate = (pair + 1 - core, occ)

    barrier = pltpu.get_barrier_semaphore()
    for step in range(1, SLICES):
        pl.semaphore_signal(barrier, inc=1, device_id=beside(step)[1], device_id_type=MESH)
    for step in range(1, 4):
        pl.semaphore_signal(barrier, inc=1, device_id=along_z(step), device_id_type=MESH)

    parts = rows // ROW_STEP

    columns = amps.shape[0]

    def load(c):
        lanes = pl.ds(pl.multiple_of(c * TILE, TILE), TILE)
        return pltpu.make_async_copy(amplitudes.at[:, lanes], amps.at[c], amp_sems.at[c])

    def load_start(c, _):
        load(c).start()
        return 0

    def load_wait(c, _):
        load(c).wait()
        return 0

    lax.fori_loop(0, columns, load_start, 0)
    tiles[4 * SLOTS] = jnp.zeros((TILE, TILE), jnp.bfloat16)
    pl.semaphore_wait(barrier, SLICES - 1 + 3)

    lane_tiles = blocks.shape[3] // TILE

    def spread_ends(to, lane):
        return (
            blocks.at[:, to, :, pl.ds(lane * TILE, TILE)],
            spread.at[pl.ds((lane_tiles * core + lane) * SHARED + 4 * y, 4)],
        )

    def spread_copy(step, lane):
        to, peer = beside(step)
        return pltpu.make_async_remote_copy(
            *spread_ends(to, lane), spread_sends.at[step, lane], spread_recvs.at[step, lane],
            device_id=peer, device_id_type=MESH,
        )

    copies = [spread_copy(step, lane) for step in range(1, SLICES) for lane in range(lane_tiles)]
    copies += [pltpu.make_async_copy(*spread_ends(me, lane), spread_recvs.at[0, lane]) for lane in range(lane_tiles)]
    for copy in copies:
        copy.start()
    for copy in copies:
        copy.wait()

    mine = pl.ds(pl.multiple_of(me * FINE, FINE), FINE)

    def pack(s, _):
        tiles[z * SLOTS + s, mine, :] = spread[pack_from[s]]
        return 0

    lax.fori_loop(0, SLOTS, pack, 0)

    def shard(origin_z, origin_y, first, count):
        at = pl.ds(lax.rem(origin_z, 4) * SLOTS + first, count)
        band = pl.ds(pl.multiple_of((2 * lax.rem(origin_y, 4) + core) * FINE, FINE), FINE)
        return tiles.at[at, band, :]

    def remote(ref, send, recv, peer):
        return pltpu.make_async_remote_copy(ref, ref, send, recv, device_id=peer, device_id_type=MESH)

    z_copies = {
        step: remote(shard(z, y, 0, SLOTS), z_sends.at[step], z_recvs.at[step], along_z(step)) for step in (1, 3, 2)
    }
    started = []

    def begin(copy):
        copy.start()
        started.append(copy)

    def landed(ref, recv):
        remote(ref, z_sends.at[0], recv, mate).wait_recv()

    def to_mate(d, e):
        begin(remote(shard(z + 4 - d, y + 4 - e, 0, SLOTS), core_sends.at[d, e], core_recvs.at[d, e], mate))

    def to_sides(d):
        ref = shard(z + 4 - d, y, 0, SLOTS)
        begin(remote(ref, y_sends.at[d, 0], y_recvs.at[d, 0], along_y(1)))
        begin(remote(ref, y_sends.at[d, 1], y_recvs.at[d, 1], along_y(3)))
        to_mate(d, 0)

    def from_sides(d):
        landed(shard(z + 4 - d, y + 3, 0, SLOTS), y_recvs.at[d, 0])
        begin(remote(shard(z + 4 - d, y + 3, 0, half), y_sends.at[d, 2], y_recvs.at[d, 2], along_y(1)))
        landed(shard(z + 4 - d, y + 1, 0, SLOTS), y_recvs.at[d, 1])
        begin(remote(shard(z + 4 - d, y + 1, half, SLOTS - half), y_sends.at[d, 3], y_recvs.at[d, 3], along_y(3)))
        to_mate(d, 1)
        to_mate(d, 3)

    def from_across(d):
        landed(shard(z + 4 - d, y + 2, 0, half), y_recvs.at[d, 2])
        landed(shard(z + 4 - d, y + 2, half, SLOTS - half), y_recvs.at[d, 3])
        to_mate(d, 2)

    def from_z(d):
        landed(shard(z + 4 - d, y, 0, SLOTS), z_recvs.at[d])
        to_sides(d)

    for step in (1, 3, 2):
        begin(z_copies[step])
    to_sides(0)
    from_z(1)
    from_z(3)
    from_sides(0)
    from_z(2)
    from_sides(1)
    from_sides(3)
    from_across(0)
    from_sides(2)
    from_across(1)
    from_across(3)
    from_across(2)
    lax.fori_loop(0, columns, load_wait, 0)
    for copy in started:
        copy.wait_send()
    for d in range(4):
        for e in range(4):
            at = pl.ds(lax.rem(z + 4 - d, 4) * SLOTS, SLOTS)
            band = pl.ds(pl.multiple_of((2 * lax.rem(y + 4 - e, 4) + 1 - core) * FINE, FINE), FINE)
            landed(tiles.at[at, band, :], core_recvs.at[d, e])

    for t in range(ladder.shape[1] // TILE):
        lanes = pl.ds(t * TILE, TILE)
        for k in range(TERMS):
            factor[pl.ds(k * TILE, TILE), :] = tiles[term_slot[t * TERMS + k]]

        def product(c, _):
            at = pl.ds(pl.multiple_of(c * ROW_STEP, ROW_STEP), ROW_STEP)
            left = jnp.concatenate(
                [amps[term_tile[t * TERMS + k], at, :] for k in range(TERMS)], axis=1
            )
            ladder[at, lanes] = jnp.dot(left, factor[...], preferred_element_type=jnp.float32)
            return 0

        lax.fori_loop(0, parts, product, 0)


def tile_lists(code):
    tiles = code.shape[0]
    number = jnp.arange(tiles, dtype=jnp.int32)
    zone, pair = number // SHARED, number // 8
    equal = code[:, None] == code[None, :]
    earlier = equal & (number[:, None] < number[None, :])
    rank = jnp.sum(earlier, axis=0, dtype=jnp.int32)
    zone_rank = jnp.sum(earlier & (zone[:, None] == zone[None, :]), axis=0, dtype=jnp.int32)
    members = jnp.sum(equal.reshape(4, SHARED, tiles), axis=1, dtype=jnp.int32)
    before = (pair[:, None] == pair[None, :]) & (number[:, None] < number[None, :])
    start = jnp.sum(jnp.where(before[None], members[:, :, None], 0), axis=1, dtype=jnp.int32)
    slot = jnp.repeat(start, SHARED, axis=0) + zone_rank[:, None]
    fits = (jnp.max(jnp.sum(members, axis=0)) <= TERMS) & (
        jnp.max(jnp.sum(members.reshape(4, tiles // 8, 8), axis=2)) <= SLOTS
    )
    return equal, rank, slot, fits


def own_lists(equal, rank, slot):
    vir, occ = lax.axis_index("vir"), lax.axis_index("occ")
    where = (occ // 4 * SHARED, vir // 2 * 8)
    kept = lax.dynamic_slice(equal, where, (SHARED, 8))
    at = jnp.where(kept, lax.dynamic_slice(slot, where, (SHARED, 8)), -1)
    hit = at[None] == jnp.arange(SLOTS, dtype=jnp.int32)[:, None, None]
    down, across = lax.broadcasted_iota(jnp.int32, (SHARED, 8), 0), lax.broadcasted_iota(jnp.int32, (SHARED, 8), 1)
    pack_from = jnp.sum(jnp.where(hit, (across * SHARED + down)[None], 0), axis=(1, 2))
    tiles = equal.shape[0]
    number = jnp.arange(tiles, dtype=jnp.int32)
    cols = (0, vir * 4)
    kept = lax.dynamic_slice(equal, cols, (tiles, 4))
    at = lax.dynamic_slice(slot, cols, (tiles, 4)) + (number // SHARED * SLOTS)[:, None]
    hit = kept[:, :, None] & (rank[:, None, None] == jnp.arange(TERMS, dtype=jnp.int32)[None, None, :])
    term_tile = jnp.sum(jnp.where(hit, number[:, None, None], 0), axis=0)
    term_slot = 4 * SLOTS + jnp.sum(jnp.where(hit, at[:, :, None] - 4 * SLOTS, 0), axis=0)
    return pack_from, term_slot.reshape(-1), term_tile.reshape(-1)


def kept_ladder(amplitudes, integrals, lists):
    rows, width = amplitudes.shape[0], integrals.shape[1]
    bf16 = jnp.bfloat16
    smem = pl.BlockSpec(memory_space=pltpu.SMEM)
    dma = pltpu.SemaphoreType.DMA
    return pl.pallas_call(
        ladder_kernel,
        out_shape=jax.ShapeDtypeStruct((rows, width), jnp.float32),
        in_specs=[smem] * 3 + [VMEM, pl.BlockSpec(memory_space=pl.ANY)],
        out_specs=VMEM,
        scratch_shapes=[
            pltpu.VMEM((2 * width // TILE * SHARED, FINE, TILE), bf16),
            pltpu.VMEM((4 * SLOTS + 1, TILE, TILE), bf16),
            pltpu.VMEM((amplitudes.shape[1] // TILE, rows, TILE), bf16),
            pltpu.VMEM((TERMS * TILE, TILE), bf16),
            dma((amplitudes.shape[1] // TILE,)),
            dma((SLICES, width // TILE)),
            dma((SLICES, width // TILE)),
            dma((4,)),
            dma((4,)),
            dma((4, 4)),
            dma((4, 4)),
            dma((4, 4)),
            dma((4, 4)),
        ],
        compiler_params=pltpu.CompilerParams(collective_id=2, has_side_effects=True, vmem_limit_bytes=48 << 20),
        name="kept_ladder",
    )(*lists, integrals.reshape(integrals.shape[0] // TILE, SLICES, FINE, width), amplitudes)


def full_ladder(amplitudes, integrals, code):
    row_count, col_count = integrals.shape
    row_tiles = row_count // TILE
    col_tiles = col_count // TILE
    row_codes = lax.dynamic_slice_in_dim(code, lax.axis_index("occ") * row_tiles, row_tiles)
    col_codes = lax.dynamic_slice_in_dim(code, lax.axis_index("vir") * col_tiles, col_tiles)
    allowed = row_codes[:, None] == col_codes[None, :]
    masked = jnp.where(
        allowed[:, None, :, None], integrals.reshape(row_tiles, TILE, col_tiles, TILE), 0
    ).reshape(row_count, col_count)
    return jnp.dot(
        amplitudes, lax.all_gather(masked, "occ", axis=0, tiled=True), preferred_element_type=jnp.float32
    )


def local(amplitudes, integrals, tile_irrep, tile_spin, row_mirror, col_mirror, occ_gap, vir_energy):
    code = tile_irrep * SPINS + tile_spin
    row_local = jnp.remainder(row_mirror, amplitudes.shape[0])
    col_local = jnp.remainder(col_mirror, integrals.shape[1])
    equal, rank, slot, fits = tile_lists(code)
    lists = own_lists(equal, rank, slot)
    ladder = lax.cond(
        fits,
        lambda: kept_ladder(amplitudes, integrals, lists),
        lambda: full_ladder(amplitudes, integrals, code),
    )
    residual = exchanged(ladder, row_local, col_local)
    return residual / (occ_gap[:, None] + vir_energy[None, :])


def solution(mesh):
    placed = (P("occ", None), P("occ", "vir"), P(), P(), P("occ"), P("vir"), P("occ"), P("vir"))
    return jax.shard_map(
        local, mesh=mesh, in_specs=placed, out_specs=P("occ", "vir"), check_vma=False
    )
```

```python
import functools
import jax
import jax.numpy as jnp
from jax import lax
from jax.sharding import PartitionSpec as P
from jax.experimental import pallas as pl
from jax.experimental.pallas import tpu as pltpu

TILE = 128
SPINS = 2
MESH = pl.DeviceIdType.MESH
CHUNK = 128
BLOCK = 512
LEVELS = 32767.0
TINY = 1e-30
SLICES = 8
FINE = TILE // SLICES
SHARED = 16
ZONES = 4
FORMS = ((40, 18),)
VMEM = pl.BlockSpec(memory_space=pltpu.VMEM)
F32, BF16 = jnp.float32, jnp.bfloat16
dot = functools.partial(jnp.dot, preferred_element_type=F32)


def span(c, size):
    return pl.ds(pl.multiple_of(c * size, size), size)


def loop(count, body):
    def step(c, _):
        body(c)
        return 0

    lax.fori_loop(0, count, step, 0)


def upright(line):
    size = line.shape[1]
    square = lax.broadcasted_iota(jnp.int32, (size, size), 0) == lax.broadcasted_iota(jnp.int32, (size, size), 1)
    return jnp.sum(jnp.where(square, line, 0), axis=1, keepdims=True, dtype=jnp.int32)


def halves(x):
    hi = x.astype(BF16)
    return hi, (x - hi.astype(F32)).astype(BF16)


def coded(x, top):
    return jnp.round(x * (LEVELS / top)).astype(jnp.int32).astype(jnp.int16)


def decoded(code, top):
    return code.astype(jnp.int32).astype(F32) * (top / LEVELS)


def place():
    vir, occ = lax.axis_index("vir"), lax.axis_index("occ")
    return vir, occ, lax.axis_size("vir"), lax.axis_size("occ")


def mirror_peers():
    vir, occ, virs, occs = place()
    return (lax.rem(vir + virs // 2, virs), occ), (vir, lax.rem(occ + occs // 2, occs))


def one_hots(row_there, col_there, to_rows, from_rows, cols):
    vir, _, virs, _ = place()
    rows, width = to_rows.shape[0], cols.shape[0]
    target = jnp.where(
        vir < virs // 2, lax.broadcasted_iota(jnp.int32, (1, width), 1), col_there[...] & (width - 1)
    )
    cols[...] = (lax.broadcasted_iota(jnp.int32, (width, width), 0) == target).astype(F32).astype(BF16)

    def make(c):
        at = span(c, CHUNK)
        down = lax.broadcasted_iota(jnp.int32, (CHUNK, rows), 0) + c * CHUNK
        to_rows[at, :] = (down == row_there[...] & (rows - 1)).astype(F32).astype(BF16)
        across = lax.broadcasted_iota(jnp.int32, (CHUNK, rows), 1)
        from_rows[at, :] = (across == upright(row_there[:, at] & (rows - 1))).astype(F32).astype(BF16)

    loop(rows // CHUNK, make)


def exchange_steps(
    ladder, out, own, there, split, out_x1, in_x1, out_z, in_z, out_x2, in_x2, tops_out, tops_in,
    to_rows, from_rows, cols, sends, recvs, top_sends, top_recvs,
):
    vir, _, virs, _ = place()
    x_peer, z_peer = mirror_peers()
    rows, width = ladder.shape
    half = width // 2
    chunks, blocks = rows // CHUNK, rows // BLOCK
    per_block = BLOCK // CHUNK
    lower = vir < virs // 2
    sign = jnp.where(lower, 1.0, -1.0).astype(F32)
    kept = pl.multiple_of(jnp.where(lower, 0, half), half)
    given = pl.multiple_of(half - kept, half)

    def tops(slot, peer):
        return pltpu.make_async_remote_copy(
            tops_out.at[slot], tops_in.at[slot], top_sends.at[slot], top_recvs.at[slot],
            device_id=peer, device_id_type=MESH,
        )

    def piece(phase, c, source, target, peer):
        at = span(c, CHUNK)
        return pltpu.make_async_remote_copy(
            source.at[at], target.at[at], sends.at[phase, c], recvs.at[phase, c], device_id=peer, device_id_type=MESH
        )

    def first(c):
        return piece(0, c, out_x1, in_x1, x_peer)

    def second(c):
        return piece(1, c, out_z, in_z, z_peer)

    def third(c):
        return piece(2, c, out_x2, in_x2, x_peer)

    def joined(x):
        return x[:, :half] + x[:, half:]

    def store_split(at, x):
        split[at, :half], split[at, half:] = halves(x)

    def in_order(columns, keep):
        wanted = cols[pl.ds(columns, half), :]

        def order(b):
            at = span(b, BLOCK)
            pair = jnp.concatenate(halves(ladder[at, :]), axis=0)
            x = lax.dot_general(pair, wanted, (((1,), (1,)), ((), ())), preferred_element_type=F32)
            x = x[:BLOCK] + x[BLOCK:]
            if keep:
                own[at, :] = x
            store_split(at, x)

        loop(blocks, order)

    in_order(given, False)

    def code_first(b):
        moved = joined(dot(to_rows[span(b, BLOCK), :], split[...]))
        for s in range(per_block):
            c = b * per_block + s
            part = moved[s * CHUNK : (s + 1) * CHUNK]
            top = jnp.maximum(jnp.max(jnp.abs(part), axis=0, keepdims=True), TINY)
            tops_out[0, pl.ds(c, 1), :] = top
            out_x1[span(c, CHUNK), :] = coded(part, top)

    loop(blocks, code_first)
    tops(0, x_peer).start()
    loop(chunks, lambda c: first(c).start())

    in_order(kept, True)

    def move_kept(b):
        moved = joined(dot(to_rows[span(b, BLOCK), :], split[...]))
        there[span(b, BLOCK), :] = moved
        for s in range(per_block):
            part = moved[s * CHUNK : (s + 1) * CHUNK]
            tops_out[1, pl.ds(b * per_block + s, 1), :] = jnp.max(jnp.abs(part), axis=0, keepdims=True)

    loop(blocks, move_kept)
    tops(0, x_peer).wait()
    tops_out[1, :, :] = tops_out[1, :, :] + tops_in[0, :, :]
    tops(1, z_peer).start()

    def send_second(c):
        at, top = span(c, CHUNK), pl.ds(c, 1)
        first(c).wait()
        came = decoded(in_x1[at, :], tops_in[0, top, :])
        store_split(at, came)
        out_z[at, :] = coded(sign * (there[at, :] - came), tops_out[1, top, :])
        second(c).start()

    loop(chunks, send_second)
    tops(1, z_peer).wait()

    def back(b):
        at = span(b, BLOCK)
        mine = sign * (own[at, :] - joined(dot(from_rows[at, :], split[...])))
        own[at, :] = mine
        for s in range(per_block):
            top = pl.ds(b * per_block + s, 1)
            part = mine[s * CHUNK : (s + 1) * CHUNK]
            tops_out[2, top, :] = jnp.max(jnp.abs(part), axis=0, keepdims=True) + tops_in[1, top, :]

    loop(blocks, back)
    tops(2, x_peer).start()

    def send_third(c):
        at, top = span(c, CHUNK), pl.ds(c, 1)
        second(c).wait()
        done = own[at, :] - decoded(in_z[at, :], tops_in[1, top, :])
        own[at, :] = done
        out_x2[at, :] = coded(done, tops_out[2, top, :])
        third(c).start()

    loop(chunks, send_third)
    tops(2, x_peer).wait()

    def finish(c):
        at = span(c, CHUNK)
        third(c).wait()
        came = decoded(in_x2[at, :], tops_in[2, pl.ds(c, 1), :])
        ours = jnp.concatenate(halves(own[at, :]), axis=0)
        theirs = jnp.concatenate(halves(came), axis=0)
        x = dot(ours, cols[pl.ds(kept, half), :]) + dot(theirs, cols[pl.ds(given, half), :])
        out[at, :] = sign * (x[:CHUNK] + x[CHUNK:])

    loop(chunks, finish)


def exchange_kernel(ladder, row_there, col_there, out, *scratch):
    barrier = pltpu.get_barrier_semaphore()
    for peer in mirror_peers():
        pl.semaphore_signal(barrier, inc=1, device_id=peer, device_id_type=MESH)
    to_rows, from_rows, cols = scratch[-7:-4]
    one_hots(row_there, col_there, to_rows, from_rows, cols)
    pl.semaphore_wait(barrier, 2)
    exchange_steps(ladder, out, *scratch)


def exchange_scratch(rows, width):
    half, chunks = width // 2, rows // CHUNK
    dma = pltpu.SemaphoreType.DMA
    return (
        [pltpu.VMEM((rows, half), F32)] * 2
        + [pltpu.VMEM((rows, width), BF16)]
        + [pltpu.VMEM((rows, half), jnp.int16)] * 6
        + [pltpu.VMEM((3, chunks, half), F32)] * 2
        + [pltpu.VMEM((rows, rows), BF16)] * 2
        + [pltpu.VMEM((width, width), BF16)]
        + [dma((3, chunks))] * 2
        + [dma((3,))] * 2
    )


def mirror_tables(row_mirror, col_mirror):
    return row_mirror[None, :], col_mirror[None, :]


def exchanged(ladder, row_mirror, col_mirror):
    return pl.pallas_call(
        exchange_kernel,
        out_shape=jax.ShapeDtypeStruct(ladder.shape, F32),
        in_specs=[VMEM] * 3,
        out_specs=VMEM,
        scratch_shapes=exchange_scratch(*ladder.shape),
        compiler_params=pltpu.CompilerParams(collective_id=1, has_side_effects=True, vmem_limit_bytes=48 << 20),
        name="exchange",
    )(ladder, *mirror_tables(row_mirror, col_mirror))


def ladder_steps(
    slots, terms, lists, blocks, amplitudes, ladder, meanwhile,
    spread, tiles, amps, factor,
    amp_sems, spread_sends, spread_recvs, z_sends, z_recvs, y_sends, y_recvs, core_sends, core_recvs,
):
    vir, occ, _, _ = place()
    core, y, z = lax.rem(vir, 2), lax.rem(occ, 4), occ // 4
    pair = vir - core
    me = 2 * y + core
    rows, width = ladder.shape
    lane_tiles = width // TILE
    columns = amps.shape[0]
    half = slots // 2

    def beside(step):
        to = lax.rem(me + step, SLICES)
        return to, (pair + lax.rem(to, 2), z * 4 + to // 2)

    def along_z(step):
        return (vir, lax.rem(z + step, 4) * 4 + y)

    def along_y(step):
        return (vir, z * 4 + lax.rem(y + step, 4))

    mate = (pair + 1 - core, occ)
    barrier = pltpu.get_barrier_semaphore()
    peers = [beside(step)[1] for step in range(1, SLICES)] + [along_z(step) for step in (1, 2, 3)] + [mirror_peers()[0]]
    for peer in peers:
        pl.semaphore_signal(barrier, inc=1, device_id=peer, device_id_type=MESH)

    def load(c):
        return pltpu.make_async_copy(amplitudes.at[:, span(c, TILE)], amps.at[c], amp_sems.at[c])

    loop(columns, lambda c: load(c).start())
    tiles[ZONES * slots] = jnp.zeros((TILE, TILE), BF16)
    pl.semaphore_wait(barrier, len(peers))

    def ends(to, lane):
        return (
            blocks.at[:, to, :, pl.ds(lane * TILE, TILE)],
            spread.at[pl.ds((lane_tiles * core + lane) * SHARED + 4 * y, 4)],
        )

    def spread_copy(step, lane):
        to, peer = beside(step)
        return pltpu.make_async_remote_copy(
            *ends(to, lane), spread_sends.at[step, lane], spread_recvs.at[step, lane],
            device_id=peer, device_id_type=MESH,
        )

    copies = [spread_copy(step, lane) for step in range(1, SLICES) for lane in range(lane_tiles)]
    copies += [pltpu.make_async_copy(*ends(me, lane), spread_recvs.at[0, lane]) for lane in range(lane_tiles)]
    for copy in copies:
        copy.start()
    meanwhile()
    for copy in copies:
        copy.wait()

    mine = span(me, FINE)

    def pack(s):
        tiles[z * slots + s, mine, :] = spread[lists[0, s]]

    loop(slots, pack)

    def shard(d, e, part, other=False):
        at = pl.ds(lax.rem(z + 4 - d, 4) * slots + part * half, half)
        owner = 2 * lax.rem(y + 4 - e, 4) + (1 - core if other else core)
        return tiles.at[at, span(owner, FINE), :]

    started = []

    def send(ref, send_sem, recv_sem, peer):
        copy = pltpu.make_async_remote_copy(ref, ref, send_sem, recv_sem, device_id=peer, device_id_type=MESH)
        copy.start()
        started.append(copy)

    def landed(ref, recv_sem):
        pltpu.make_async_remote_copy(
            ref, ref, z_sends.at[0, 0], recv_sem, device_id=mate, device_id_type=MESH
        ).wait_recv()

    def to_mate(d, e, part):
        send(shard(d, e, part), core_sends.at[d, e, part], core_recvs.at[d, e, part], mate)

    def z_out(part):
        for step in (1, 3):
            send(shard(0, 0, part), z_sends.at[step, part], z_recvs.at[step, part], along_z(step))

    def y_out(d, part):
        for step in (1, 3):
            send(shard(d, 0, part), y_sends.at[d, step, part], y_recvs.at[d, step, part], along_y(step))
        to_mate(d, 0, part)

    def z_in(part):
        near, far = (1, 3) if part == 0 else (3, 1)
        landed(shard(near, 0, part), z_recvs.at[near, part])
        send(shard(near, 0, part), z_sends.at[2, part], z_recvs.at[2, part], along_z(near))
        y_out(near, part)
        landed(shard(far, 0, part), z_recvs.at[far, part])
        y_out(far, part)

    def z_across(part):
        landed(shard(2, 0, part), z_recvs.at[2, part])
        y_out(2, part)

    def y_in(d, part):
        near, far = (1, 3) if part == 0 else (3, 1)
        landed(shard(d, near, part), y_recvs.at[d, near, part])
        send(shard(d, near, part), y_sends.at[d, 2, part], y_recvs.at[d, 2, part], along_y(near))
        to_mate(d, near, part)
        landed(shard(d, far, part), y_recvs.at[d, far, part])
        to_mate(d, far, part)

    def y_across(d, part):
        landed(shard(d, 2, part), y_recvs.at[d, 2, part])
        to_mate(d, 2, part)

    for part in (0, 1):
        z_out(part)
        y_out(0, part)
    y_in(0, 0)
    y_in(0, 1)
    z_in(0)
    y_across(0, 0)
    z_in(1)
    y_across(0, 1)
    y_in(1, 0)
    y_in(3, 0)
    z_across(0)
    y_in(3, 1)
    y_in(1, 1)
    z_across(1)
    for d, part in ((1, 0), (3, 0), (3, 1), (1, 1)):
        y_across(d, part)
    y_in(2, 0)
    y_in(2, 1)
    y_across(2, 0)
    y_across(2, 1)
    loop(columns, lambda c: load(c).wait())
    for copy in started:
        copy.wait_send()
    for d in range(4):
        for e in range(4):
            for part in (0, 1):
                landed(shard(d, e, part, True), core_recvs.at[d, e, part])

    for t in range(lane_tiles):
        for k in range(terms):
            factor[pl.ds(k * TILE, TILE), :] = tiles[lists[1 + t, k]]

        def product(b):
            at = span(b, BLOCK // 2)
            left = jnp.concatenate([amps[lists[1 + lane_tiles + t, k], at, :] for k in range(terms)], axis=1)
            ladder[at, pl.ds(t * TILE, TILE)] = dot(left, factor[...])

        loop(rows // (BLOCK // 2), product)


def ladder_scratch(rows, summed, width, slots, terms):
    dma = pltpu.SemaphoreType.DMA
    return [
        pltpu.VMEM((2 * width // TILE * SHARED, FINE, TILE), BF16),
        pltpu.VMEM((ZONES * slots + 1, TILE, TILE), BF16),
        pltpu.VMEM((summed // TILE, rows, TILE), BF16),
        pltpu.VMEM((terms * TILE, TILE), BF16),
        dma((summed // TILE,)),
        dma((SLICES, width // TILE)),
        dma((SLICES, width // TILE)),
        dma((4, 2)),
        dma((4, 2)),
        dma((4, 4, 2)),
        dma((4, 4, 2)),
        dma((4, 4, 2)),
        dma((4, 4, 2)),
    ]


def fused_kernel(slots, terms, count, lists, row_there, col_there, blocks, amplitudes, out, ladder, *scratch):
    swap = scratch[:count]
    meanwhile = functools.partial(one_hots, row_there, col_there, *swap[-7:-4])
    ladder_steps(slots, terms, lists, blocks, amplitudes, ladder, meanwhile, *scratch[count:])
    exchange_steps(ladder, out, *swap)


def packed(form, lists, amplitudes, integrals, row_mirror, col_mirror):
    slots, terms = FORMS[form]
    (rows, summed), width = amplitudes.shape, integrals.shape[1]
    swap = exchange_scratch(rows, width)
    return pl.pallas_call(
        functools.partial(fused_kernel, slots, terms, len(swap)),
        out_shape=jax.ShapeDtypeStruct((rows, width), F32),
        in_specs=[pl.BlockSpec(memory_space=pltpu.SMEM)] + [VMEM] * 3 + [pl.BlockSpec(memory_space=pl.ANY)],
        out_specs=VMEM,
        scratch_shapes=[pltpu.VMEM((rows, width), F32)] + swap + ladder_scratch(rows, summed, width, slots, terms),
        compiler_params=pltpu.CompilerParams(
            collective_id=2 + form, has_side_effects=True, vmem_limit_bytes=56 << 20
        ),
        name="packed",
    )(
        lists,
        *mirror_tables(row_mirror, col_mirror),
        integrals.reshape(integrals.shape[0] // TILE, SLICES, FINE, width),
        amplitudes,
    )


def lists_kernel(irrep, spin, lists):
    vir, occ, _, _ = place()
    across = irrep[...] * SPINS + spin[...]
    down = upright(across)
    tiles = down.shape[0]
    number = lax.broadcasted_iota(jnp.int32, (tiles, tiles), 0)
    other = lax.broadcasted_iota(jnp.int32, (tiles, tiles), 1)
    equal = down == across
    one = jnp.where(equal, 1, 0)
    prior = jnp.where(other < number, one, 0)
    total = functools.partial(jnp.sum, keepdims=True, dtype=jnp.int32)
    rank = total(prior, axis=1)
    zone_rank = total(jnp.where(other // SHARED == number // SHARED, prior, 0), axis=1)
    before = (number < other) & (number // 8 == other // 8)
    slot = zone_rank + jnp.zeros((tiles, tiles), jnp.int32)
    widest = jnp.zeros((1, 1), jnp.int32)
    for zone in range(ZONES):
        members = total(jnp.where(other // SHARED == zone, one, 0), axis=1)
        start = total(jnp.where(before, members, 0), axis=0)
        slot += jnp.where(number // SHARED == zone, start, 0)
        group = total(jnp.where(number // 8 == other // 8, members, 0), axis=0)
        widest = jnp.maximum(widest, jnp.max(group, axis=1, keepdims=True))
    longest = jnp.max(total(one, axis=0), axis=1, keepdims=True)
    form = jnp.full((1, 1), len(FORMS), jnp.int32)
    stride = jnp.zeros((1, 1), jnp.int32)
    for f, (slots, terms) in reversed(list(enumerate(FORMS))):
        fits = (widest <= slots) & (longest <= terms)
        form = jnp.where(fits, f, form)
        stride = jnp.where(fits, slots, stride)

    entry = lax.broadcasted_iota(jnp.int32, (tiles, TILE), 1)
    tile = lax.broadcasted_iota(jnp.int32, (tiles, TILE), 0)

    def column(x, a):
        return total(jnp.where(other == a, x, 0), axis=1)

    pack = jnp.zeros((1, TILE), jnp.int32)
    here = tile // SHARED == occ // 4
    for a in range(8):
        hit = here & (column(one, vir // 2 * 8 + a) == 1) & (column(slot, vir // 2 * 8 + a) == entry)
        pack += total(jnp.where(hit, a * SHARED + tile % SHARED, 0), axis=0)
    lists[0:1, :] = pack
    for t in range(4):
        a = vir * 4 + t
        hit = (column(one, a) == 1) & (rank == entry)
        at = tile // SHARED * stride + column(slot, a) - ZONES * stride
        lists[1 + t : 2 + t, :] = ZONES * stride + total(jnp.where(hit, at, 0), axis=0)
        lists[5 + t : 6 + t, :] = total(jnp.where(hit, tile, 0), axis=0)
    lists[9:10, :] = form + jnp.zeros((1, TILE), jnp.int32)


def tile_lists(tile_irrep, tile_spin):
    return pl.pallas_call(
        lists_kernel,
        out_shape=jax.ShapeDtypeStruct((16, TILE), jnp.int32),
        in_specs=[VMEM] * 2,
        out_specs=VMEM,
        name="lists",
    )(tile_irrep[None, :], tile_spin[None, :])


def full_ladder(amplitudes, integrals, code):
    row_count, col_count = integrals.shape
    row_tiles = row_count // TILE
    col_tiles = col_count // TILE
    row_codes = lax.dynamic_slice_in_dim(code, lax.axis_index("occ") * row_tiles, row_tiles)
    col_codes = lax.dynamic_slice_in_dim(code, lax.axis_index("vir") * col_tiles, col_tiles)
    allowed = row_codes[:, None] == col_codes[None, :]
    masked = jnp.where(
        allowed[:, None, :, None], integrals.reshape(row_tiles, TILE, col_tiles, TILE), 0
    ).reshape(row_count, col_count)
    return jnp.dot(amplitudes, lax.all_gather(masked, "occ", axis=0, tiled=True), preferred_element_type=F32)


def local(amplitudes, integrals, tile_irrep, tile_spin, row_mirror, col_mirror, occ_gap, vir_energy):
    lists = tile_lists(tile_irrep, tile_spin)

    def whole():
        ladder = full_ladder(amplitudes, integrals, tile_irrep * SPINS + tile_spin)
        return exchanged(ladder, row_mirror, col_mirror)

    forms = [
        functools.partial(packed, form, lists, amplitudes, integrals, row_mirror, col_mirror)
        for form in range(len(FORMS))
    ]
    residual = lax.switch(lists[9, 0], forms + [whole])
    return residual / (occ_gap[:, None] + vir_energy[None, :])


def solution(mesh):
    placed = (P("occ", None), P("occ", "vir"), P(), P(), P("occ"), P("vir"), P("occ"), P("vir"))
    return jax.shard_map(local, mesh=mesh, in_specs=placed, out_specs=P("occ", "vir"), check_vma=False)
```

```python
import functools
import jax
import jax.numpy as jnp
from jax import lax
from jax.sharding import PartitionSpec as P
from jax.experimental import pallas as pl
from jax.experimental.pallas import tpu as pltpu

TILE = 128
SPINS = 2
MESH = pl.DeviceIdType.MESH
CHUNK = 128
BLOCK = 512
LEVELS = 32767.0
TINY = 1e-30
SLICES = 8
FINE = TILE // SLICES
SHARED = 16
ZONES = 4
FORMS = ((28, 14), (34, 16), (52, 22))
VMEM = pl.BlockSpec(memory_space=pltpu.VMEM)
F32, BF16 = jnp.float32, jnp.bfloat16
dot = functools.partial(jnp.dot, preferred_element_type=F32)


def span(c, size):
    return pl.ds(pl.multiple_of(c * size, size), size)


def loop(count, body):
    def step(c, _):
        body(c)
        return 0

    lax.fori_loop(0, count, step, 0)


def upright(line):
    size = line.shape[1]
    square = lax.broadcasted_iota(jnp.int32, (size, size), 0) == lax.broadcasted_iota(jnp.int32, (size, size), 1)
    return jnp.sum(jnp.where(square, line, 0), axis=1, keepdims=True, dtype=jnp.int32)


def halves(x):
    hi = x.astype(BF16)
    return hi, (x - hi.astype(F32)).astype(BF16)


def coded(x, top):
    return jnp.round(x * (LEVELS / top)).astype(jnp.int32).astype(jnp.int16)


def decoded(code, top):
    return code.astype(jnp.int32).astype(F32) * (top / LEVELS)


def place():
    vir, occ = lax.axis_index("vir"), lax.axis_index("occ")
    return vir, occ, lax.axis_size("vir"), lax.axis_size("occ")


def mirror_peers():
    vir, occ, virs, occs = place()
    return (lax.rem(vir + virs // 2, virs), occ), (vir, lax.rem(occ + occs // 2, occs))


def one_hots(row_there, col_there, to_rows, from_rows, cols):
    vir, _, virs, _ = place()
    rows, width = to_rows.shape[0], cols.shape[0]
    target = jnp.where(
        vir < virs // 2, lax.broadcasted_iota(jnp.int32, (1, width), 1), col_there[...] & (width - 1)
    )
    cols[...] = (lax.broadcasted_iota(jnp.int32, (width, width), 0) == target).astype(F32).astype(BF16)

    def make(c):
        at = span(c, CHUNK)
        down = lax.broadcasted_iota(jnp.int32, (CHUNK, rows), 0) + c * CHUNK
        to_rows[at, :] = (down == row_there[...] & (rows - 1)).astype(F32).astype(BF16)
        across = lax.broadcasted_iota(jnp.int32, (CHUNK, rows), 1)
        from_rows[at, :] = (across == upright(row_there[:, at] & (rows - 1))).astype(F32).astype(BF16)

    loop(rows // CHUNK, make)


def exchange_steps(
    ladder, out, own, there, split, out_x1, in_x1, out_z, in_z, out_x2, in_x2, tops_out, tops_in,
    to_rows, from_rows, cols, sends, recvs, top_sends, top_recvs,
):
    vir, _, virs, _ = place()
    x_peer, z_peer = mirror_peers()
    rows, width = ladder.shape
    half = width // 2
    chunks, blocks = rows // CHUNK, rows // BLOCK
    per_block = BLOCK // CHUNK
    lower = vir < virs // 2
    sign = jnp.where(lower, 1.0, -1.0).astype(F32)
    kept = pl.multiple_of(jnp.where(lower, 0, half), half)
    given = pl.multiple_of(half - kept, half)

    def tops(slot, peer):
        return pltpu.make_async_remote_copy(
            tops_out.at[slot], tops_in.at[slot], top_sends.at[slot], top_recvs.at[slot],
            device_id=peer, device_id_type=MESH,
        )

    def piece(phase, c, source, target, peer):
        at = span(c, CHUNK)
        return pltpu.make_async_remote_copy(
            source.at[at], target.at[at], sends.at[phase, c], recvs.at[phase, c], device_id=peer, device_id_type=MESH
        )

    def first(c):
        return piece(0, c, out_x1, in_x1, x_peer)

    def second(c):
        return piece(1, c, out_z, in_z, z_peer)

    def third(c):
        return piece(2, c, out_x2, in_x2, x_peer)

    def joined(x):
        return x[:, :half] + x[:, half:]

    def store_split(at, x):
        split[at, :half], split[at, half:] = halves(x)

    def in_order(columns, keep):
        wanted = cols[pl.ds(columns, half), :]

        def order(b):
            at = span(b, BLOCK)
            pair = jnp.concatenate(halves(ladder[at, :]), axis=0)
            x = lax.dot_general(pair, wanted, (((1,), (1,)), ((), ())), preferred_element_type=F32)
            x = x[:BLOCK] + x[BLOCK:]
            if keep:
                own[at, :] = x
            store_split(at, x)

        loop(blocks, order)

    in_order(given, False)

    def code_first(b):
        moved = joined(dot(to_rows[span(b, BLOCK), :], split[...]))
        for s in range(per_block):
            c = b * per_block + s
            part = moved[s * CHUNK : (s + 1) * CHUNK]
            top = jnp.maximum(jnp.max(jnp.abs(part), axis=0, keepdims=True), TINY)
            tops_out[0, pl.ds(c, 1), :] = top
            out_x1[span(c, CHUNK), :] = coded(part, top)

    loop(blocks, code_first)
    tops(0, x_peer).start()
    loop(chunks, lambda c: first(c).start())

    in_order(kept, True)

    def move_kept(b):
        moved = joined(dot(to_rows[span(b, BLOCK), :], split[...]))
        there[span(b, BLOCK), :] = moved
        for s in range(per_block):
            part = moved[s * CHUNK : (s + 1) * CHUNK]
            tops_out[1, pl.ds(b * per_block + s, 1), :] = jnp.max(jnp.abs(part), axis=0, keepdims=True)

    loop(blocks, move_kept)
    tops(0, x_peer).wait()
    tops_out[1, :, :] = tops_out[1, :, :] + tops_in[0, :, :]
    tops(1, z_peer).start()

    def send_second(c):
        at, top = span(c, CHUNK), pl.ds(c, 1)
        first(c).wait()
        came = decoded(in_x1[at, :], tops_in[0, top, :])
        store_split(at, came)
        out_z[at, :] = coded(sign * (there[at, :] - came), tops_out[1, top, :])
        second(c).start()

    loop(chunks, send_second)
    tops(1, z_peer).wait()

    def back(b):
        at = span(b, BLOCK)
        mine = sign * (own[at, :] - joined(dot(from_rows[at, :], split[...])))
        own[at, :] = mine
        for s in range(per_block):
            top = pl.ds(b * per_block + s, 1)
            part = mine[s * CHUNK : (s + 1) * CHUNK]
            tops_out[2, top, :] = jnp.max(jnp.abs(part), axis=0, keepdims=True) + tops_in[1, top, :]

    loop(blocks, back)
    tops(2, x_peer).start()

    def send_third(c):
        at, top = span(c, CHUNK), pl.ds(c, 1)
        second(c).wait()
        done = own[at, :] - decoded(in_z[at, :], tops_in[1, top, :])
        own[at, :] = done
        out_x2[at, :] = coded(done, tops_out[2, top, :])
        third(c).start()

    loop(chunks, send_third)
    tops(2, x_peer).wait()

    def finish(c):
        at = span(c, CHUNK)
        third(c).wait()
        came = decoded(in_x2[at, :], tops_in[2, pl.ds(c, 1), :])
        ours = jnp.concatenate(halves(own[at, :]), axis=0)
        theirs = jnp.concatenate(halves(came), axis=0)
        x = dot(ours, cols[pl.ds(kept, half), :]) + dot(theirs, cols[pl.ds(given, half), :])
        out[at, :] = sign * (x[:CHUNK] + x[CHUNK:])

    loop(chunks, finish)


def exchange_kernel(ladder, row_there, col_there, out, *scratch):
    barrier = pltpu.get_barrier_semaphore()
    for peer in mirror_peers():
        pl.semaphore_signal(barrier, inc=1, device_id=peer, device_id_type=MESH)
    to_rows, from_rows, cols = scratch[-7:-4]
    one_hots(row_there, col_there, to_rows, from_rows, cols)
    pl.semaphore_wait(barrier, 2)
    exchange_steps(ladder, out, *scratch)


def exchange_scratch(rows, width):
    half, chunks = width // 2, rows // CHUNK
    dma = pltpu.SemaphoreType.DMA
    return (
        [pltpu.VMEM((rows, half), F32)] * 2
        + [pltpu.VMEM((rows, width), BF16)]
        + [pltpu.VMEM((rows, half), jnp.int16)] * 6
        + [pltpu.VMEM((3, chunks, half), F32)] * 2
        + [pltpu.VMEM((rows, rows), BF16)] * 2
        + [pltpu.VMEM((width, width), BF16)]
        + [dma((3, chunks))] * 2
        + [dma((3,))] * 2
    )


def mirror_tables(row_mirror, col_mirror):
    return row_mirror[None, :], col_mirror[None, :]


def exchanged(ladder, row_mirror, col_mirror):
    return pl.pallas_call(
        exchange_kernel,
        out_shape=jax.ShapeDtypeStruct(ladder.shape, F32),
        in_specs=[VMEM] * 3,
        out_specs=VMEM,
        scratch_shapes=exchange_scratch(*ladder.shape),
        compiler_params=pltpu.CompilerParams(collective_id=1, has_side_effects=True, vmem_limit_bytes=48 << 20),
        name="exchange",
    )(ladder, *mirror_tables(row_mirror, col_mirror))


def ladder_steps(
    slots, terms, lists, blocks, amplitudes, ladder, meanwhile,
    spread, tiles, amps, factor,
    amp_sems, spread_sends, spread_recvs, z_sends, z_recvs, y_sends, y_recvs, core_sends, core_recvs,
):
    vir, occ, _, _ = place()
    core, y, z = lax.rem(vir, 2), lax.rem(occ, 4), occ // 4
    pair = vir - core
    me = 2 * y + core
    rows, width = ladder.shape
    lane_tiles = width // TILE
    columns = amps.shape[0]
    half = slots // 2

    def beside(step):
        to = lax.rem(me + step, SLICES)
        return to, (pair + lax.rem(to, 2), z * 4 + to // 2)

    def along_z(step):
        return (vir, lax.rem(z + step, 4) * 4 + y)

    def along_y(step):
        return (vir, z * 4 + lax.rem(y + step, 4))

    mate = (pair + 1 - core, occ)
    barrier = pltpu.get_barrier_semaphore()
    peers = [beside(step)[1] for step in range(1, SLICES)] + [along_z(step) for step in (1, 2, 3)] + [mirror_peers()[0]]
    for peer in peers:
        pl.semaphore_signal(barrier, inc=1, device_id=peer, device_id_type=MESH)

    def load(c):
        return pltpu.make_async_copy(amplitudes.at[:, span(c, TILE)], amps.at[c], amp_sems.at[c])

    loop(columns, lambda c: load(c).start())
    tiles[ZONES * slots] = jnp.zeros((TILE, TILE), BF16)
    pl.semaphore_wait(barrier, len(peers))

    def ends(to, lane):
        return (
            blocks.at[:, to, :, pl.ds(lane * TILE, TILE)],
            spread.at[pl.ds((lane_tiles * core + lane) * SHARED + 4 * y, 4)],
        )

    def spread_copy(step, lane):
        to, peer = beside(step)
        return pltpu.make_async_remote_copy(
            *ends(to, lane), spread_sends.at[step, lane], spread_recvs.at[step, lane],
            device_id=peer, device_id_type=MESH,
        )

    copies = [spread_copy(step, lane) for step in range(1, SLICES) for lane in range(lane_tiles)]
    copies += [pltpu.make_async_copy(*ends(me, lane), spread_recvs.at[0, lane]) for lane in range(lane_tiles)]
    for copy in copies:
        copy.start()
    meanwhile()
    for copy in copies:
        copy.wait()

    mine = span(me, FINE)

    def pack(s):
        tiles[z * slots + s, mine, :] = spread[lists[0, s]]

    loop(slots, pack)

    def shard(d, e, part, other=False):
        at = pl.ds(lax.rem(z + 4 - d, 4) * slots + part * half, half)
        owner = 2 * lax.rem(y + 4 - e, 4) + (1 - core if other else core)
        return tiles.at[at, span(owner, FINE), :]

    started = []

    def send(ref, send_sem, recv_sem, peer):
        copy = pltpu.make_async_remote_copy(ref, ref, send_sem, recv_sem, device_id=peer, device_id_type=MESH)
        copy.start()
        started.append(copy)

    def landed(ref, recv_sem):
        pltpu.make_async_remote_copy(
            ref, ref, z_sends.at[0, 0], recv_sem, device_id=mate, device_id_type=MESH
        ).wait_recv()

    def to_mate(d, e, part):
        send(shard(d, e, part), core_sends.at[d, e, part], core_recvs.at[d, e, part], mate)

    def z_out(part):
        for step in (1, 3):
            send(shard(0, 0, part), z_sends.at[step, part], z_recvs.at[step, part], along_z(step))

    def y_out(d, part):
        for step in (1, 3):
            send(shard(d, 0, part), y_sends.at[d, step, part], y_recvs.at[d, step, part], along_y(step))
        to_mate(d, 0, part)

    def z_in(part):
        near, far = (1, 3) if part == 0 else (3, 1)
        landed(shard(near, 0, part), z_recvs.at[near, part])
        send(shard(near, 0, part), z_sends.at[2, part], z_recvs.at[2, part], along_z(near))
        y_out(near, part)
        landed(shard(far, 0, part), z_recvs.at[far, part])
        y_out(far, part)

    def z_across(part):
        landed(shard(2, 0, part), z_recvs.at[2, part])
        y_out(2, part)

    def y_in(d, part):
        near, far = (1, 3) if part == 0 else (3, 1)
        landed(shard(d, near, part), y_recvs.at[d, near, part])
        send(shard(d, near, part), y_sends.at[d, 2, part], y_recvs.at[d, 2, part], along_y(near))
        to_mate(d, near, part)
        landed(shard(d, far, part), y_recvs.at[d, far, part])
        to_mate(d, far, part)

    def y_across(d, part):
        landed(shard(d, 2, part), y_recvs.at[d, 2, part])
        to_mate(d, 2, part)

    for part in (0, 1):
        z_out(part)
        y_out(0, part)
    y_in(0, 0)
    y_in(0, 1)
    z_in(0)
    y_across(0, 0)
    z_in(1)
    y_across(0, 1)
    y_in(1, 0)
    y_in(3, 0)
    z_across(0)
    y_in(3, 1)
    y_in(1, 1)
    z_across(1)
    for d, part in ((1, 0), (3, 0), (3, 1), (1, 1)):
        y_across(d, part)
    y_in(2, 0)
    y_in(2, 1)
    y_across(2, 0)
    y_across(2, 1)
    loop(columns, lambda c: load(c).wait())
    for copy in started:
        copy.wait_send()
    for d in range(4):
        for e in range(4):
            for part in (0, 1):
                landed(shard(d, e, part, True), core_recvs.at[d, e, part])

    for t in range(lane_tiles):
        for k in range(terms):
            factor[pl.ds(k * TILE, TILE), :] = tiles[lists[1 + t, k]]

        left = jnp.concatenate([amps[lists[1 + lane_tiles + t, k]] for k in range(terms)], axis=1)
        ladder[:, pl.ds(t * TILE, TILE)] = dot(left, factor[...])


def ladder_scratch(rows, summed, width, slots, terms):
    dma = pltpu.SemaphoreType.DMA
    return [
        pltpu.VMEM((2 * width // TILE * SHARED, FINE, TILE), BF16),
        pltpu.VMEM((ZONES * slots + 1, TILE, TILE), BF16),
        pltpu.VMEM((summed // TILE, rows, TILE), BF16),
        pltpu.VMEM((terms * TILE, TILE), BF16),
        dma((summed // TILE,)),
        dma((SLICES, width // TILE)),
        dma((SLICES, width // TILE)),
        dma((4, 2)),
        dma((4, 2)),
        dma((4, 4, 2)),
        dma((4, 4, 2)),
        dma((4, 4, 2)),
        dma((4, 4, 2)),
    ]


def fused_kernel(slots, terms, count, lists, row_there, col_there, blocks, amplitudes, out, ladder, *scratch):
    swap = scratch[:count]
    meanwhile = functools.partial(one_hots, row_there, col_there, *swap[-7:-4])
    ladder_steps(slots, terms, lists, blocks, amplitudes, ladder, meanwhile, *scratch[count:])
    exchange_steps(ladder, out, *swap)


def packed(form, lists, amplitudes, integrals, row_mirror, col_mirror):
    slots, terms = FORMS[form]
    (rows, summed), width = amplitudes.shape, integrals.shape[1]
    swap = exchange_scratch(rows, width)
    return pl.pallas_call(
        functools.partial(fused_kernel, slots, terms, len(swap)),
        out_shape=jax.ShapeDtypeStruct((rows, width), F32),
        in_specs=[pl.BlockSpec(memory_space=pltpu.SMEM)] + [VMEM] * 3 + [pl.BlockSpec(memory_space=pl.ANY)],
        out_specs=VMEM,
        scratch_shapes=[pltpu.VMEM((rows, width), F32)] + swap + ladder_scratch(rows, summed, width, slots, terms),
        compiler_params=pltpu.CompilerParams(
            collective_id=2 + form, has_side_effects=True, vmem_limit_bytes=56 << 20
        ),
        name="packed",
    )(
        lists,
        *mirror_tables(row_mirror, col_mirror),
        integrals.reshape(integrals.shape[0] // TILE, SLICES, FINE, width),
        amplitudes,
    )


def lists_kernel(irrep, spin, lists):
    vir, occ, _, _ = place()
    across = irrep[...] * SPINS + spin[...]
    down = upright(across)
    tiles = down.shape[0]
    number = lax.broadcasted_iota(jnp.int32, (tiles, tiles), 0)
    other = lax.broadcasted_iota(jnp.int32, (tiles, tiles), 1)
    equal = down == across
    one = jnp.where(equal, 1, 0)
    prior = jnp.where(other < number, one, 0)
    total = functools.partial(jnp.sum, keepdims=True, dtype=jnp.int32)
    rank = total(prior, axis=1)
    zone_rank = total(jnp.where(other // SHARED == number // SHARED, prior, 0), axis=1)
    before = (number < other) & (number // 8 == other // 8)
    slot = zone_rank + jnp.zeros((tiles, tiles), jnp.int32)
    widest = jnp.zeros((1, 1), jnp.int32)
    for zone in range(ZONES):
        members = total(jnp.where(other // SHARED == zone, one, 0), axis=1)
        start = total(jnp.where(before, members, 0), axis=0)
        slot += jnp.where(number // SHARED == zone, start, 0)
        group = total(jnp.where(number // 8 == other // 8, members, 0), axis=0)
        widest = jnp.maximum(widest, jnp.max(group, axis=1, keepdims=True))
    longest = jnp.max(total(one, axis=0), axis=1, keepdims=True)
    form = jnp.full((1, 1), len(FORMS), jnp.int32)
    stride = jnp.zeros((1, 1), jnp.int32)
    for f, (slots, terms) in reversed(list(enumerate(FORMS))):
        fits = (widest <= slots) & (longest <= terms)
        form = jnp.where(fits, f, form)
        stride = jnp.where(fits, slots, stride)

    entry = lax.broadcasted_iota(jnp.int32, (tiles, TILE), 1)
    tile = lax.broadcasted_iota(jnp.int32, (tiles, TILE), 0)

    def column(x, a):
        return total(jnp.where(other == a, x, 0), axis=1)

    pack = jnp.zeros((1, TILE), jnp.int32)
    here = tile // SHARED == occ // 4
    for a in range(8):
        hit = here & (column(one, vir // 2 * 8 + a) == 1) & (column(slot, vir // 2 * 8 + a) == entry)
        pack += total(jnp.where(hit, a * SHARED + tile % SHARED, 0), axis=0)
    lists[0:1, :] = pack
    for t in range(4):
        a = vir * 4 + t
        hit = (column(one, a) == 1) & (rank == entry)
        at = tile // SHARED * stride + column(slot, a) - ZONES * stride
        lists[1 + t : 2 + t, :] = ZONES * stride + total(jnp.where(hit, at, 0), axis=0)
        lists[5 + t : 6 + t, :] = total(jnp.where(hit, tile, 0), axis=0)
    lists[9:10, :] = form + jnp.zeros((1, TILE), jnp.int32)


def tile_lists(tile_irrep, tile_spin):
    return pl.pallas_call(
        lists_kernel,
        out_shape=jax.ShapeDtypeStruct((16, TILE), jnp.int32),
        in_specs=[VMEM] * 2,
        out_specs=VMEM,
        name="lists",
    )(tile_irrep[None, :], tile_spin[None, :])


def full_ladder(amplitudes, integrals, code):
    row_count, col_count = integrals.shape
    row_tiles = row_count // TILE
    col_tiles = col_count // TILE
    row_codes = lax.dynamic_slice_in_dim(code, lax.axis_index("occ") * row_tiles, row_tiles)
    col_codes = lax.dynamic_slice_in_dim(code, lax.axis_index("vir") * col_tiles, col_tiles)
    allowed = row_codes[:, None] == col_codes[None, :]
    masked = jnp.where(
        allowed[:, None, :, None], integrals.reshape(row_tiles, TILE, col_tiles, TILE), 0
    ).reshape(row_count, col_count)
    return jnp.dot(amplitudes, lax.all_gather(masked, "occ", axis=0, tiled=True), preferred_element_type=F32)


def local(amplitudes, integrals, tile_irrep, tile_spin, row_mirror, col_mirror, occ_gap, vir_energy):
    lists = tile_lists(tile_irrep, tile_spin)

    def whole():
        ladder = full_ladder(amplitudes, integrals, tile_irrep * SPINS + tile_spin)
        return exchanged(ladder, row_mirror, col_mirror)

    forms = [
        functools.partial(packed, form, lists, amplitudes, integrals, row_mirror, col_mirror)
        for form in range(len(FORMS))
    ]
    residual = lax.switch(lists[9, 0], forms + [whole])
    return residual / (occ_gap[:, None] + vir_energy[None, :])


def solution(mesh):
    placed = (P("occ", None), P("occ", "vir"), P(), P(), P("occ"), P("vir"), P("occ"), P("vir"))
    return jax.shard_map(local, mesh=mesh, in_specs=placed, out_specs=P("occ", "vir"), check_vma=False)
```

```python
import functools
import jax
import jax.numpy as jnp
from jax import lax
from jax.sharding import PartitionSpec as P
from jax.experimental import pallas as pl
from jax.experimental.pallas import tpu as pltpu

TILE = 128
SPINS = 2
MESH = pl.DeviceIdType.MESH
CHUNK = 128
BLOCK = 512
LEVELS = 32767.0
TINY = 1e-30
SLICES = 8
FINE = TILE // SLICES
SHARED = 16
ZONES = 4
FORMS = ((28, 14), (32, 16), (38, 18), (56, 24))
VMEM = pl.BlockSpec(memory_space=pltpu.VMEM)
F32, BF16 = jnp.float32, jnp.bfloat16
dot = functools.partial(jnp.dot, preferred_element_type=F32)


def span(c, size):
    return pl.ds(pl.multiple_of(c * size, size), size)


def loop(count, body):
    def step(c, _):
        body(c)
        return 0

    lax.fori_loop(0, count, step, 0)


def upright(line):
    size = line.shape[1]
    square = lax.broadcasted_iota(jnp.int32, (size, size), 0) == lax.broadcasted_iota(jnp.int32, (size, size), 1)
    return jnp.sum(jnp.where(square, line, 0), axis=1, keepdims=True, dtype=jnp.int32)


def halves(x):
    hi = x.astype(BF16)
    return hi, (x - hi.astype(F32)).astype(BF16)


def coded(x, top):
    return jnp.round(x * (LEVELS / top)).astype(jnp.int32).astype(jnp.int16)


def decoded(code, top):
    return code.astype(jnp.int32).astype(F32) * (top / LEVELS)


def place():
    vir, occ = lax.axis_index("vir"), lax.axis_index("occ")
    return vir, occ, lax.axis_size("vir"), lax.axis_size("occ")


def mirror_peers():
    vir, occ, virs, occs = place()
    return (lax.rem(vir + virs // 2, virs), occ), (vir, lax.rem(occ + occs // 2, occs))


def one_hots(row_there, col_there, to_rows, from_rows, cols):
    vir, _, virs, _ = place()
    rows, width = to_rows.shape[0], cols.shape[0]
    target = jnp.where(
        vir < virs // 2, lax.broadcasted_iota(jnp.int32, (1, width), 1), col_there[...] & (width - 1)
    )
    cols[...] = (lax.broadcasted_iota(jnp.int32, (width, width), 0) == target).astype(F32).astype(BF16)

    def make(c):
        at = span(c, CHUNK)
        down = lax.broadcasted_iota(jnp.int32, (CHUNK, rows), 0) + c * CHUNK
        to_rows[at, :] = (down == row_there[...] & (rows - 1)).astype(F32).astype(BF16)
        across = lax.broadcasted_iota(jnp.int32, (CHUNK, rows), 1)
        from_rows[at, :] = (across == upright(row_there[:, at] & (rows - 1))).astype(F32).astype(BF16)

    loop(rows // CHUNK, make)


def exchange_steps(
    ladder, out, own, there, split, out_x1, in_x1, out_z, in_z, out_x2, in_x2, tops_out, tops_in,
    to_rows, from_rows, cols, sends, recvs, top_sends, top_recvs,
):
    vir, _, virs, _ = place()
    x_peer, z_peer = mirror_peers()
    rows, width = ladder.shape
    half = width // 2
    chunks, blocks = rows // CHUNK, rows // BLOCK
    per_block = BLOCK // CHUNK
    lower = vir < virs // 2
    sign = jnp.where(lower, 1.0, -1.0).astype(F32)
    kept = pl.multiple_of(jnp.where(lower, 0, half), half)
    given = pl.multiple_of(half - kept, half)

    def tops(slot, peer):
        return pltpu.make_async_remote_copy(
            tops_out.at[slot], tops_in.at[slot], top_sends.at[slot], top_recvs.at[slot],
            device_id=peer, device_id_type=MESH,
        )

    def piece(phase, c, source, target, peer):
        at = span(c, CHUNK)
        return pltpu.make_async_remote_copy(
            source.at[at], target.at[at], sends.at[phase, c], recvs.at[phase, c], device_id=peer, device_id_type=MESH
        )

    def first(c):
        return piece(0, c, out_x1, in_x1, x_peer)

    def second(c):
        return piece(1, c, out_z, in_z, z_peer)

    def third(c):
        return piece(2, c, out_x2, in_x2, x_peer)

    def joined(x):
        return x[:, :half] + x[:, half:]

    def store_split(at, x):
        split[at, :half], split[at, half:] = halves(x)

    def in_order(columns, keep):
        wanted = cols[pl.ds(columns, half), :]

        def order(b):
            at = span(b, BLOCK)
            pair = jnp.concatenate(halves(ladder[at, :]), axis=0)
            x = lax.dot_general(pair, wanted, (((1,), (1,)), ((), ())), preferred_element_type=F32)
            x = x[:BLOCK] + x[BLOCK:]
            if keep:
                own[at, :] = x
            store_split(at, x)

        loop(blocks, order)

    in_order(given, False)

    def code_first(b):
        moved = joined(dot(to_rows[span(b, BLOCK), :], split[...]))
        for s in range(per_block):
            c = b * per_block + s
            part = moved[s * CHUNK : (s + 1) * CHUNK]
            top = jnp.maximum(jnp.max(jnp.abs(part), axis=0, keepdims=True), TINY)
            tops_out[0, pl.ds(c, 1), :] = top
            out_x1[span(c, CHUNK), :] = coded(part, top)

    loop(blocks, code_first)
    tops(0, x_peer).start()
    loop(chunks, lambda c: first(c).start())

    in_order(kept, True)

    def move_kept(b):
        moved = joined(dot(to_rows[span(b, BLOCK), :], split[...]))
        there[span(b, BLOCK), :] = moved
        for s in range(per_block):
            part = moved[s * CHUNK : (s + 1) * CHUNK]
            tops_out[1, pl.ds(b * per_block + s, 1), :] = jnp.max(jnp.abs(part), axis=0, keepdims=True)

    loop(blocks, move_kept)
    tops(0, x_peer).wait()
    tops_out[1, :, :] = tops_out[1, :, :] + tops_in[0, :, :]
    tops(1, z_peer).start()

    def send_second(c):
        at, top = span(c, CHUNK), pl.ds(c, 1)
        first(c).wait()
        came = decoded(in_x1[at, :], tops_in[0, top, :])
        store_split(at, came)
        out_z[at, :] = coded(sign * (there[at, :] - came), tops_out[1, top, :])
        second(c).start()

    loop(chunks, send_second)
    tops(1, z_peer).wait()

    def back(b):
        at = span(b, BLOCK)
        mine = sign * (own[at, :] - joined(dot(from_rows[at, :], split[...])))
        own[at, :] = mine
        for s in range(per_block):
            top = pl.ds(b * per_block + s, 1)
            part = mine[s * CHUNK : (s + 1) * CHUNK]
            tops_out[2, top, :] = jnp.max(jnp.abs(part), axis=0, keepdims=True) + tops_in[1, top, :]

    loop(blocks, back)
    tops(2, x_peer).start()

    def send_third(c):
        at, top = span(c, CHUNK), pl.ds(c, 1)
        second(c).wait()
        done = own[at, :] - decoded(in_z[at, :], tops_in[1, top, :])
        own[at, :] = done
        out_x2[at, :] = coded(done, tops_out[2, top, :])
        third(c).start()

    loop(chunks, send_third)
    tops(2, x_peer).wait()

    def finish(c):
        at = span(c, CHUNK)
        third(c).wait()
        came = decoded(in_x2[at, :], tops_in[2, pl.ds(c, 1), :])
        ours = jnp.concatenate(halves(own[at, :]), axis=0)
        theirs = jnp.concatenate(halves(came), axis=0)
        x = dot(ours, cols[pl.ds(kept, half), :]) + dot(theirs, cols[pl.ds(given, half), :])
        out[at, :] = sign * (x[:CHUNK] + x[CHUNK:])

    loop(chunks, finish)


def exchange_kernel(ladder, row_there, col_there, out, *scratch):
    barrier = pltpu.get_barrier_semaphore()
    for peer in mirror_peers():
        pl.semaphore_signal(barrier, inc=1, device_id=peer, device_id_type=MESH)
    to_rows, from_rows, cols = scratch[-7:-4]
    one_hots(row_there, col_there, to_rows, from_rows, cols)
    pl.semaphore_wait(barrier, 2)
    exchange_steps(ladder, out, *scratch)


def exchange_scratch(rows, width):
    half, chunks = width // 2, rows // CHUNK
    dma = pltpu.SemaphoreType.DMA
    return (
        [pltpu.VMEM((rows, half), F32)] * 2
        + [pltpu.VMEM((rows, width), BF16)]
        + [pltpu.VMEM((rows, half), jnp.int16)] * 6
        + [pltpu.VMEM((3, chunks, half), F32)] * 2
        + [pltpu.VMEM((rows, rows), BF16)] * 2
        + [pltpu.VMEM((width, width), BF16)]
        + [dma((3, chunks))] * 2
        + [dma((3,))] * 2
    )


def mirror_tables(row_mirror, col_mirror):
    return row_mirror[None, :], col_mirror[None, :]


def exchanged(ladder, row_mirror, col_mirror):
    return pl.pallas_call(
        exchange_kernel,
        out_shape=jax.ShapeDtypeStruct(ladder.shape, F32),
        in_specs=[VMEM] * 3,
        out_specs=VMEM,
        scratch_shapes=exchange_scratch(*ladder.shape),
        compiler_params=pltpu.CompilerParams(collective_id=1, has_side_effects=True, vmem_limit_bytes=48 << 20),
        name="exchange",
    )(ladder, *mirror_tables(row_mirror, col_mirror))


def ladder_steps(
    slots, terms, lists, blocks, amplitudes, ladder, meanwhile,
    spread, tiles, amps, factor,
    amp_sems, spread_sends, spread_recvs, z_sends, z_recvs, y_sends, y_recvs, core_sends, core_recvs,
):
    vir, occ, _, _ = place()
    core, y, z = lax.rem(vir, 2), lax.rem(occ, 4), occ // 4
    pair = vir - core
    me = 2 * y + core
    rows, width = ladder.shape
    lane_tiles = width // TILE
    columns = amps.shape[0]
    half = slots // 2

    def beside(step):
        to = lax.rem(me + step, SLICES)
        return to, (pair + lax.rem(to, 2), z * 4 + to // 2)

    def along_z(step):
        return (vir, lax.rem(z + step, 4) * 4 + y)

    def along_y(step):
        return (vir, z * 4 + lax.rem(y + step, 4))

    mate = (pair + 1 - core, occ)
    barrier = pltpu.get_barrier_semaphore()
    peers = [beside(step)[1] for step in range(1, SLICES)] + [along_z(step) for step in (1, 2, 3)] + [mirror_peers()[0]]
    for peer in peers:
        pl.semaphore_signal(barrier, inc=1, device_id=peer, device_id_type=MESH)

    def load(c):
        return pltpu.make_async_copy(amplitudes.at[:, span(c, TILE)], amps.at[c], amp_sems.at[c])

    loop(columns, lambda c: load(c).start())
    tiles[ZONES * slots] = jnp.zeros((TILE, TILE), BF16)
    pl.semaphore_wait(barrier, len(peers))

    def ends(to, lane):
        return (
            blocks.at[:, to, :, pl.ds(lane * TILE, TILE)],
            spread.at[pl.ds((lane_tiles * core + lane) * SHARED + 4 * y, 4)],
        )

    def spread_copy(step, lane):
        to, peer = beside(step)
        return pltpu.make_async_remote_copy(
            *ends(to, lane), spread_sends.at[step, lane], spread_recvs.at[step, lane],
            device_id=peer, device_id_type=MESH,
        )

    copies = [spread_copy(step, lane) for step in range(1, SLICES) for lane in range(lane_tiles)]
    copies += [pltpu.make_async_copy(*ends(me, lane), spread_recvs.at[0, lane]) for lane in range(lane_tiles)]
    for copy in copies:
        copy.start()
    meanwhile()
    for copy in copies:
        copy.wait()

    mine = span(me, FINE)

    def pack(s):
        tiles[z * slots + s, mine, :] = spread[lists[0, s]]

    loop(slots, pack)

    def shard(d, e, part, other=False):
        at = pl.ds(lax.rem(z + 4 - d, 4) * slots + part * half, half)
        owner = 2 * lax.rem(y + 4 - e, 4) + (1 - core if other else core)
        return tiles.at[at, span(owner, FINE), :]

    started = []

    def send(ref, send_sem, recv_sem, peer):
        copy = pltpu.make_async_remote_copy(ref, ref, send_sem, recv_sem, device_id=peer, device_id_type=MESH)
        copy.start()
        started.append(copy)

    def landed(ref, recv_sem):
        pltpu.make_async_remote_copy(
            ref, ref, z_sends.at[0, 0], recv_sem, device_id=mate, device_id_type=MESH
        ).wait_recv()

    def to_mate(d, e, part):
        send(shard(d, e, part), core_sends.at[d, e, part], core_recvs.at[d, e, part], mate)

    def z_out(part):
        for step in (1, 3):
            send(shard(0, 0, part), z_sends.at[step, part], z_recvs.at[step, part], along_z(step))

    def y_out(d, part):
        for step in (1, 3):
            send(shard(d, 0, part), y_sends.at[d, step, part], y_recvs.at[d, step, part], along_y(step))
        to_mate(d, 0, part)

    def z_in(part):
        near, far = (1, 3) if part == 0 else (3, 1)
        landed(shard(near, 0, part), z_recvs.at[near, part])
        send(shard(near, 0, part), z_sends.at[2, part], z_recvs.at[2, part], along_z(near))
        y_out(near, part)
        landed(shard(far, 0, part), z_recvs.at[far, part])
        y_out(far, part)

    def z_across(part):
        landed(shard(2, 0, part), z_recvs.at[2, part])
        y_out(2, part)

    def y_in(d, part):
        near, far = (1, 3) if part == 0 else (3, 1)
        landed(shard(d, near, part), y_recvs.at[d, near, part])
        send(shard(d, near, part), y_sends.at[d, 2, part], y_recvs.at[d, 2, part], along_y(near))
        to_mate(d, near, part)
        landed(shard(d, far, part), y_recvs.at[d, far, part])
        to_mate(d, far, part)

    def y_across(d, part):
        landed(shard(d, 2, part), y_recvs.at[d, 2, part])
        to_mate(d, 2, part)

    for part in (0, 1):
        z_out(part)
        y_out(0, part)
    y_in(0, 0)
    y_in(0, 1)
    z_in(0)
    y_across(0, 0)
    z_in(1)
    y_across(0, 1)
    y_in(1, 0)
    y_in(3, 0)
    z_across(0)
    y_in(3, 1)
    y_in(1, 1)
    z_across(1)
    for d, part in ((1, 0), (3, 0), (3, 1), (1, 1)):
        y_across(d, part)
    y_in(2, 0)
    y_in(2, 1)
    y_across(2, 0)
    y_across(2, 1)
    loop(columns, lambda c: load(c).wait())
    for copy in started:
        copy.wait_send()
    for d in range(4):
        for e in range(4):
            for part in (0, 1):
                landed(shard(d, e, part, True), core_recvs.at[d, e, part])

    for t in range(lane_tiles):
        for k in range(terms):
            factor[pl.ds(k * TILE, TILE), :] = tiles[lists[1 + t, k]]

        left = jnp.concatenate([amps[lists[1 + lane_tiles + t, k]] for k in range(terms)], axis=1)
        ladder[:, pl.ds(t * TILE, TILE)] = dot(left, factor[...])


def ladder_scratch(rows, summed, width, slots, terms):
    dma = pltpu.SemaphoreType.DMA
    return [
        pltpu.VMEM((2 * width // TILE * SHARED, FINE, TILE), BF16),
        pltpu.VMEM((ZONES * slots + 1, TILE, TILE), BF16),
        pltpu.VMEM((summed // TILE, rows, TILE), BF16),
        pltpu.VMEM((terms * TILE, TILE), BF16),
        dma((summed // TILE,)),
        dma((SLICES, width // TILE)),
        dma((SLICES, width // TILE)),
        dma((4, 2)),
        dma((4, 2)),
        dma((4, 4, 2)),
        dma((4, 4, 2)),
        dma((4, 4, 2)),
        dma((4, 4, 2)),
    ]


def fused_kernel(slots, terms, count, lists, row_there, col_there, blocks, amplitudes, out, ladder, *scratch):
    swap = scratch[:count]
    meanwhile = functools.partial(one_hots, row_there, col_there, *swap[-7:-4])
    ladder_steps(slots, terms, lists, blocks, amplitudes, ladder, meanwhile, *scratch[count:])
    exchange_steps(ladder, out, *swap)


def packed(form, lists, amplitudes, integrals, row_mirror, col_mirror):
    slots, terms = FORMS[form]
    (rows, summed), width = amplitudes.shape, integrals.shape[1]
    swap = exchange_scratch(rows, width)
    return pl.pallas_call(
        functools.partial(fused_kernel, slots, terms, len(swap)),
        out_shape=jax.ShapeDtypeStruct((rows, width), F32),
        in_specs=[pl.BlockSpec(memory_space=pltpu.SMEM)] + [VMEM] * 3 + [pl.BlockSpec(memory_space=pl.ANY)],
        out_specs=VMEM,
        scratch_shapes=[pltpu.VMEM((rows, width), F32)] + swap + ladder_scratch(rows, summed, width, slots, terms),
        compiler_params=pltpu.CompilerParams(
            collective_id=2 + form, has_side_effects=True, vmem_limit_bytes=56 << 20
        ),
        name="packed",
    )(
        lists,
        *mirror_tables(row_mirror, col_mirror),
        integrals.reshape(integrals.shape[0] // TILE, SLICES, FINE, width),
        amplitudes,
    )


def lists_kernel(irrep, spin, lists, chosen):
    vir, occ, _, _ = place()
    across = irrep[...] * SPINS + spin[...]
    down = upright(across)
    tiles = down.shape[0]
    number = lax.broadcasted_iota(jnp.int32, (tiles, tiles), 0)
    other = lax.broadcasted_iota(jnp.int32, (tiles, tiles), 1)
    equal = down == across
    one = jnp.where(equal, 1, 0)
    prior = jnp.where(other < number, one, 0)
    total = functools.partial(jnp.sum, keepdims=True, dtype=jnp.int32)
    rank = total(prior, axis=1)
    zone_rank = total(jnp.where(other // SHARED == number // SHARED, prior, 0), axis=1)
    before = (number < other) & (number // 8 == other // 8)
    slot = zone_rank + jnp.zeros((tiles, tiles), jnp.int32)
    widest = jnp.zeros((1, 1), jnp.int32)
    for zone in range(ZONES):
        members = total(jnp.where(other // SHARED == zone, one, 0), axis=1)
        start = total(jnp.where(before, members, 0), axis=0)
        slot += jnp.where(number // SHARED == zone, start, 0)
        group = total(jnp.where(number // 8 == other // 8, members, 0), axis=0)
        widest = jnp.maximum(widest, jnp.max(group, axis=1, keepdims=True))
    longest = jnp.max(total(one, axis=0), axis=1, keepdims=True)
    form = jnp.full((1, 1), len(FORMS), jnp.int32)
    stride = jnp.zeros((1, 1), jnp.int32)
    for f, (slots, terms) in reversed(list(enumerate(FORMS))):
        fits = (widest <= slots) & (longest <= terms)
        form = jnp.where(fits, f, form)
        stride = jnp.where(fits, slots, stride)

    entry = lax.broadcasted_iota(jnp.int32, (tiles, TILE), 1)
    tile = lax.broadcasted_iota(jnp.int32, (tiles, TILE), 0)

    def column(x, a):
        return total(jnp.where(other == a, x, 0), axis=1)

    pack = jnp.zeros((1, TILE), jnp.int32)
    here = tile // SHARED == occ // 4
    for a in range(8):
        hit = here & (column(one, vir // 2 * 8 + a) == 1) & (column(slot, vir // 2 * 8 + a) == entry)
        pack += total(jnp.where(hit, a * SHARED + tile % SHARED, 0), axis=0)
    lists[0:1, :] = pack
    for t in range(4):
        a = vir * 4 + t
        hit = (column(one, a) == 1) & (rank == entry)
        at = tile // SHARED * stride + column(slot, a) - ZONES * stride
        lists[1 + t : 2 + t, :] = ZONES * stride + total(jnp.where(hit, at, 0), axis=0)
        lists[5 + t : 6 + t, :] = total(jnp.where(hit, tile, 0), axis=0)
    chosen[0, 0] = jnp.max(form)


def tile_lists(tile_irrep, tile_spin):
    return pl.pallas_call(
        lists_kernel,
        out_shape=(jax.ShapeDtypeStruct((16, TILE), jnp.int32), jax.ShapeDtypeStruct((1, 1), jnp.int32)),
        in_specs=[VMEM] * 2,
        out_specs=(VMEM, pl.BlockSpec(memory_space=pltpu.SMEM)),
        name="lists",
    )(tile_irrep[None, :], tile_spin[None, :])


def full_ladder(amplitudes, integrals, code):
    row_count, col_count = integrals.shape
    row_tiles = row_count // TILE
    col_tiles = col_count // TILE
    row_codes = lax.dynamic_slice_in_dim(code, lax.axis_index("occ") * row_tiles, row_tiles)
    col_codes = lax.dynamic_slice_in_dim(code, lax.axis_index("vir") * col_tiles, col_tiles)
    allowed = row_codes[:, None] == col_codes[None, :]
    masked = jnp.where(
        allowed[:, None, :, None], integrals.reshape(row_tiles, TILE, col_tiles, TILE), 0
    ).reshape(row_count, col_count)
    return jnp.dot(amplitudes, lax.all_gather(masked, "occ", axis=0, tiled=True), preferred_element_type=F32)


def local(amplitudes, integrals, tile_irrep, tile_spin, row_mirror, col_mirror, occ_gap, vir_energy):
    lists, chosen = tile_lists(tile_irrep, tile_spin)

    def whole():
        ladder = full_ladder(amplitudes, integrals, tile_irrep * SPINS + tile_spin)
        return exchanged(ladder, row_mirror, col_mirror)

    forms = [
        functools.partial(packed, form, lists, amplitudes, integrals, row_mirror, col_mirror)
        for form in range(len(FORMS))
    ]
    residual = lax.switch(chosen[0, 0], forms + [whole])
    return residual / (occ_gap[:, None] + vir_energy[None, :])


def solution(mesh):
    placed = (P("occ", None), P("occ", "vir"), P(), P(), P("occ"), P("vir"), P("occ"), P("vir"))
    return jax.shard_map(local, mesh=mesh, in_specs=placed, out_specs=P("occ", "vir"), check_vma=False)
```

```python
import functools
import jax
import jax.numpy as jnp
from jax import lax
from jax.sharding import PartitionSpec as P
from jax.experimental import pallas as pl
from jax.experimental.pallas import tpu as pltpu

TILE = 128
SPINS = 2
MESH = pl.DeviceIdType.MESH
CHUNK = 128
BLOCK = 512
LEVELS = 32767.0
TINY = 1e-30
SLICES = 8
FINE = TILE // SLICES
SHARED = 16
ZONES = 4
FORMS = ((28, 6, 14), (32, 6, 16), (38, 8, 18), (56, 10, 24))
VMEM = pl.BlockSpec(memory_space=pltpu.VMEM)
F32, BF16 = jnp.float32, jnp.bfloat16
dot = functools.partial(jnp.dot, preferred_element_type=F32)


def span(c, size):
    return pl.ds(pl.multiple_of(c * size, size), size)


def loop(count, body):
    def step(c, _):
        body(c)
        return 0

    lax.fori_loop(0, count, step, 0)


def upright(line):
    size = line.shape[1]
    square = lax.broadcasted_iota(jnp.int32, (size, size), 0) == lax.broadcasted_iota(jnp.int32, (size, size), 1)
    return jnp.sum(jnp.where(square, line, 0), axis=1, keepdims=True, dtype=jnp.int32)


def halves(x):
    hi = x.astype(BF16)
    return hi, (x - hi.astype(F32)).astype(BF16)


def coded(x, top):
    return jnp.round(x * (LEVELS / top)).astype(jnp.int32).astype(jnp.int16)


def decoded(code, top):
    return code.astype(jnp.int32).astype(F32) * (top / LEVELS)


def place():
    vir, occ = lax.axis_index("vir"), lax.axis_index("occ")
    return vir, occ, lax.axis_size("vir"), lax.axis_size("occ")


def mirror_peers():
    vir, occ, virs, occs = place()
    return (lax.rem(vir + virs // 2, virs), occ), (vir, lax.rem(occ + occs // 2, occs))


def one_hots(row_there, col_there, to_rows, from_rows, cols):
    vir, _, virs, _ = place()
    rows, width = to_rows.shape[0], cols.shape[0]
    target = jnp.where(
        vir < virs // 2, lax.broadcasted_iota(jnp.int32, (1, width), 1), col_there[...] & (width - 1)
    )
    cols[...] = (lax.broadcasted_iota(jnp.int32, (width, width), 0) == target).astype(F32).astype(BF16)

    def make(c):
        at = span(c, CHUNK)
        down = lax.broadcasted_iota(jnp.int32, (CHUNK, rows), 0) + c * CHUNK
        to_rows[at, :] = (down == row_there[...] & (rows - 1)).astype(F32).astype(BF16)
        across = lax.broadcasted_iota(jnp.int32, (CHUNK, rows), 1)
        from_rows[at, :] = (across == upright(row_there[:, at] & (rows - 1))).astype(F32).astype(BF16)

    loop(rows // CHUNK, make)


def exchange_steps(
    ladder, out, own, there, split, out_x1, in_x1, out_z, in_z, out_x2, in_x2, tops_out, tops_in,
    to_rows, from_rows, cols, sends, recvs, top_sends, top_recvs,
):
    vir, _, virs, _ = place()
    x_peer, z_peer = mirror_peers()
    rows, width = ladder.shape
    half = width // 2
    chunks, blocks = rows // CHUNK, rows // BLOCK
    per_block = BLOCK // CHUNK
    lower = vir < virs // 2
    sign = jnp.where(lower, 1.0, -1.0).astype(F32)
    kept = pl.multiple_of(jnp.where(lower, 0, half), half)
    given = pl.multiple_of(half - kept, half)

    def tops(slot, peer):
        return pltpu.make_async_remote_copy(
            tops_out.at[slot], tops_in.at[slot], top_sends.at[slot], top_recvs.at[slot],
            device_id=peer, device_id_type=MESH,
        )

    def piece(phase, c, source, target, peer):
        at = span(c, CHUNK)
        return pltpu.make_async_remote_copy(
            source.at[at], target.at[at], sends.at[phase, c], recvs.at[phase, c], device_id=peer, device_id_type=MESH
        )

    def first(c):
        return piece(0, c, out_x1, in_x1, x_peer)

    def second(c):
        return piece(1, c, out_z, in_z, z_peer)

    def third(c):
        return piece(2, c, out_x2, in_x2, x_peer)

    def joined(x):
        return x[:, :half] + x[:, half:]

    def store_split(at, x):
        split[at, :half], split[at, half:] = halves(x)

    def in_order(columns, keep):
        wanted = cols[pl.ds(columns, half), :]

        def order(b):
            at = span(b, BLOCK)
            pair = jnp.concatenate(halves(ladder[at, :]), axis=0)
            x = lax.dot_general(pair, wanted, (((1,), (1,)), ((), ())), preferred_element_type=F32)
            x = x[:BLOCK] + x[BLOCK:]
            if keep:
                own[at, :] = x
            store_split(at, x)

        loop(blocks, order)

    in_order(given, False)

    def code_first(b):
        moved = joined(dot(to_rows[span(b, BLOCK), :], split[...]))
        for s in range(per_block):
            c = b * per_block + s
            part = moved[s * CHUNK : (s + 1) * CHUNK]
            top = jnp.maximum(jnp.max(jnp.abs(part), axis=0, keepdims=True), TINY)
            tops_out[0, pl.ds(c, 1), :] = top
            out_x1[span(c, CHUNK), :] = coded(part, top)

    loop(blocks, code_first)
    tops(0, x_peer).start()
    loop(chunks, lambda c: first(c).start())

    in_order(kept, True)

    def move_kept(b):
        moved = joined(dot(to_rows[span(b, BLOCK), :], split[...]))
        there[span(b, BLOCK), :] = moved
        for s in range(per_block):
            part = moved[s * CHUNK : (s + 1) * CHUNK]
            tops_out[1, pl.ds(b * per_block + s, 1), :] = jnp.max(jnp.abs(part), axis=0, keepdims=True)

    loop(blocks, move_kept)
    tops(0, x_peer).wait()
    tops_out[1, :, :] = tops_out[1, :, :] + tops_in[0, :, :]
    tops(1, z_peer).start()

    def send_second(c):
        at, top = span(c, CHUNK), pl.ds(c, 1)
        first(c).wait()
        came = decoded(in_x1[at, :], tops_in[0, top, :])
        store_split(at, came)
        out_z[at, :] = coded(sign * (there[at, :] - came), tops_out[1, top, :])
        second(c).start()

    loop(chunks, send_second)
    tops(1, z_peer).wait()

    def back(b):
        at = span(b, BLOCK)
        mine = sign * (own[at, :] - joined(dot(from_rows[at, :], split[...])))
        own[at, :] = mine
        for s in range(per_block):
            top = pl.ds(b * per_block + s, 1)
            part = mine[s * CHUNK : (s + 1) * CHUNK]
            tops_out[2, top, :] = jnp.max(jnp.abs(part), axis=0, keepdims=True) + tops_in[1, top, :]

    loop(blocks, back)
    tops(2, x_peer).start()

    def send_third(c):
        at, top = span(c, CHUNK), pl.ds(c, 1)
        second(c).wait()
        done = own[at, :] - decoded(in_z[at, :], tops_in[1, top, :])
        own[at, :] = done
        out_x2[at, :] = coded(done, tops_out[2, top, :])
        third(c).start()

    loop(chunks, send_third)
    tops(2, x_peer).wait()

    def finish(c):
        at = span(c, CHUNK)
        third(c).wait()
        came = decoded(in_x2[at, :], tops_in[2, pl.ds(c, 1), :])
        ours = jnp.concatenate(halves(own[at, :]), axis=0)
        theirs = jnp.concatenate(halves(came), axis=0)
        x = dot(ours, cols[pl.ds(kept, half), :]) + dot(theirs, cols[pl.ds(given, half), :])
        out[at, :] = sign * (x[:CHUNK] + x[CHUNK:])

    loop(chunks, finish)


def exchange_kernel(ladder, row_there, col_there, out, *scratch):
    barrier = pltpu.get_barrier_semaphore()
    for peer in mirror_peers():
        pl.semaphore_signal(barrier, inc=1, device_id=peer, device_id_type=MESH)
    to_rows, from_rows, cols = scratch[-7:-4]
    one_hots(row_there, col_there, to_rows, from_rows, cols)
    pl.semaphore_wait(barrier, 2)
    exchange_steps(ladder, out, *scratch)


def exchange_scratch(rows, width):
    half, chunks = width // 2, rows // CHUNK
    dma = pltpu.SemaphoreType.DMA
    return (
        [pltpu.VMEM((rows, half), F32)] * 2
        + [pltpu.VMEM((rows, width), BF16)]
        + [pltpu.VMEM((rows, half), jnp.int16)] * 6
        + [pltpu.VMEM((3, chunks, half), F32)] * 2
        + [pltpu.VMEM((rows, rows), BF16)] * 2
        + [pltpu.VMEM((width, width), BF16)]
        + [dma((3, chunks))] * 2
        + [dma((3,))] * 2
    )


def mirror_tables(row_mirror, col_mirror):
    return row_mirror[None, :], col_mirror[None, :]


def exchanged(ladder, row_mirror, col_mirror):
    return pl.pallas_call(
        exchange_kernel,
        out_shape=jax.ShapeDtypeStruct(ladder.shape, F32),
        in_specs=[VMEM] * 3,
        out_specs=VMEM,
        scratch_shapes=exchange_scratch(*ladder.shape),
        compiler_params=pltpu.CompilerParams(collective_id=1, has_side_effects=True, vmem_limit_bytes=48 << 20),
        name="exchange",
    )(ladder, *mirror_tables(row_mirror, col_mirror))


def ladder_steps(
    slots, early, terms, lists, blocks, amplitudes, ladder, meanwhile,
    spread, tiles, amps, factor,
    amp_sems, spread_sends, spread_recvs, z_sends, z_recvs, y_sends, y_recvs, core_sends, core_recvs,
):
    vir, occ, _, _ = place()
    core, y, z = lax.rem(vir, 2), lax.rem(occ, 4), occ // 4
    pair = vir - core
    me = 4 * core + y
    rows, width = ladder.shape
    lane_tiles = width // TILE
    columns = amps.shape[0]
    late = slots - early
    half, small = late // 2, early // 2

    def beside(step):
        to = lax.rem(me + step, SLICES)
        return to, (pair + to // 4, z * 4 + lax.rem(to, 4))

    def along_z(step):
        return (vir, lax.rem(z + step, 4) * 4 + y)

    def along_y(step):
        return (vir, z * 4 + lax.rem(y + step, 4))

    mate = (pair + 1 - core, occ)
    barrier = pltpu.get_barrier_semaphore()
    peers = [beside(step)[1] for step in range(1, SLICES)] + [along_z(step) for step in (1, 2, 3)] + [mirror_peers()[0]]
    for peer in peers:
        pl.semaphore_signal(barrier, inc=1, device_id=peer, device_id_type=MESH)

    def load(c):
        return pltpu.make_async_copy(amplitudes.at[:, span(c, TILE)], amps.at[c], amp_sems.at[c])

    loop(columns, lambda c: load(c).start())
    for owner in range(SLICES):
        tiles[owner, ZONES * slots] = jnp.zeros((FINE, TILE), BF16)
    pl.semaphore_wait(barrier, len(peers))

    def ends(to, lane):
        return (
            blocks.at[:, to, :, pl.ds(lane * TILE, TILE)],
            spread.at[pl.ds((lane_tiles * core + lane) * SHARED + 4 * y, 4)],
        )

    def spread_copy(step, lane):
        to, peer = beside(step)
        return pltpu.make_async_remote_copy(
            *ends(to, lane), spread_sends.at[step, lane], spread_recvs.at[step, lane],
            device_id=peer, device_id_type=MESH,
        )

    copies = [spread_copy(step, lane) for step in range(1, SLICES) for lane in range(lane_tiles)]
    copies += [pltpu.make_async_copy(*ends(me, lane), spread_recvs.at[0, lane]) for lane in range(lane_tiles)]
    for copy in copies:
        copy.start()
    meanwhile()
    for copy in copies:
        copy.wait()

    def pack(s):
        tiles[me, z * slots + s] = spread[lists[0, s]]

    loop(slots, pack)

    def shard(d, e, part, other=False):
        at = pl.ds(lax.rem(z + 4 - d, 4) * slots + part * half, half)
        owner = 4 * (1 - core if other else core) + lax.rem(y + 4 - e, 4)
        return tiles.at[owner, at]

    def early_at(d, part):
        return pl.ds(lax.rem(z + 4 - d, 4) * slots + late + part * small, small)

    def early_shard(e, part, other=False):
        return tiles.at[4 * (1 - core if other else core) + lax.rem(y + 4 - e, 4), early_at(0, part)]

    def early_ring(d, part, other=False):
        return tiles.at[pl.ds(4 * (1 - core if other else core), 4), early_at(d, part)]

    started = []

    def send(ref, send_sem, recv_sem, peer):
        copy = pltpu.make_async_remote_copy(ref, ref, send_sem, recv_sem, device_id=peer, device_id_type=MESH)
        copy.start()
        started.append(copy)

    def landed(ref, recv_sem):
        pltpu.make_async_remote_copy(
            ref, ref, z_sends.at[0, 0], recv_sem, device_id=mate, device_id_type=MESH
        ).wait_recv()

    def to_mate(d, e, part):
        send(shard(d, e, part), core_sends.at[d, e, part], core_recvs.at[d, e, part], mate)

    def z_out(part):
        for step in (1, 3):
            send(shard(0, 0, part), z_sends.at[step, part], z_recvs.at[step, part], along_z(step))

    def y_out(d, part):
        for step in (1, 3):
            send(shard(d, 0, part), y_sends.at[d, step, part], y_recvs.at[d, step, part], along_y(step))
        to_mate(d, 0, part)

    def z_in(part):
        near, far = (1, 3) if part == 0 else (3, 1)
        landed(shard(near, 0, part), z_recvs.at[near, part])
        send(shard(near, 0, part), z_sends.at[2, part], z_recvs.at[2, part], along_z(near))
        y_out(near, part)
        landed(shard(far, 0, part), z_recvs.at[far, part])
        y_out(far, part)

    def z_across(part):
        landed(shard(2, 0, part), z_recvs.at[2, part])
        y_out(2, part)

    def y_in(d, part):
        near, far = (1, 3) if part == 0 else (3, 1)
        landed(shard(d, near, part), y_recvs.at[d, near, part])
        send(shard(d, near, part), y_sends.at[d, 2, part], y_recvs.at[d, 2, part], along_y(near))
        to_mate(d, near, part)
        landed(shard(d, far, part), y_recvs.at[d, far, part])
        to_mate(d, far, part)

    def y_across(d, part):
        landed(shard(d, 2, part), y_recvs.at[d, 2, part])
        to_mate(d, 2, part)

    def early_to_mate(e, part):
        send(early_shard(e, part), core_sends.at[4, e, part], core_recvs.at[4, e, part], mate)

    def ring_to_mate(d, part):
        send(early_ring(d, part), core_sends.at[5, d, part], core_recvs.at[5, d, part], mate)

    def early_out(part):
        for step in (1, 3):
            send(early_shard(0, part), y_sends.at[4, step, part], y_recvs.at[4, step, part], along_y(step))
        early_to_mate(0, part)

    def early_in(part):
        near, far = (1, 3) if part == 0 else (3, 1)
        landed(early_shard(near, part), y_recvs.at[4, near, part])
        send(early_shard(near, part), y_sends.at[4, 2, part], y_recvs.at[4, 2, part], along_y(near))
        early_to_mate(near, part)
        landed(early_shard(far, part), y_recvs.at[4, far, part])
        early_to_mate(far, part)

    def ring_out(part):
        landed(early_shard(2, part), y_recvs.at[4, 2, part])
        early_to_mate(2, part)
        for step in (1, 3):
            send(early_ring(0, part), z_sends.at[4 + step, part], z_recvs.at[4 + step, part], along_z(step))

    def ring_in(part):
        near, far = (1, 3) if part == 0 else (3, 1)
        landed(early_ring(near, part), z_recvs.at[4 + near, part])
        send(early_ring(near, part), z_sends.at[6, part], z_recvs.at[6, part], along_z(near))
        ring_to_mate(near, part)
        landed(early_ring(far, part), z_recvs.at[4 + far, part])
        ring_to_mate(far, part)

    def ring_across(part):
        landed(early_ring(2, part), z_recvs.at[6, part])
        ring_to_mate(2, part)

    for part in (0, 1):
        z_out(part)
        early_out(part)
    for part in (0, 1):
        y_out(0, part)
    early_in(0)
    early_in(1)
    y_in(0, 0)
    ring_out(0)
    ring_out(1)
    y_in(0, 1)
    z_in(0)
    y_across(0, 0)
    z_in(1)
    y_across(0, 1)
    y_in(1, 0)
    y_in(3, 0)
    z_across(0)
    y_in(3, 1)
    y_in(1, 1)
    z_across(1)
    ring_in(0)
    ring_in(1)
    for d, part in ((1, 0), (3, 0), (3, 1), (1, 1)):
        y_across(d, part)
    y_in(2, 0)
    y_in(2, 1)
    ring_across(0)
    ring_across(1)
    y_across(2, 0)
    y_across(2, 1)
    loop(columns, lambda c: load(c).wait())
    for copy in started:
        copy.wait_send()
    for d in range(4):
        for e in range(4):
            for part in (0, 1):
                landed(shard(d, e, part, True), core_recvs.at[d, e, part])
    for d in range(4):
        for part in (0, 1):
            landed(early_shard(d, part, True), core_recvs.at[4, d, part])
            if d > 0:
                landed(early_ring(d, part, True), core_recvs.at[5, d, part])

    for t in range(lane_tiles):
        for k in range(terms):
            for owner in range(SLICES):
                factor[pl.ds(k * TILE + owner * FINE, FINE), :] = tiles[owner, lists[1 + t, k]]

        left = jnp.concatenate([amps[lists[1 + lane_tiles + t, k]] for k in range(terms)], axis=1)
        ladder[:, pl.ds(t * TILE, TILE)] = dot(left, factor[...])


def ladder_scratch(rows, summed, width, slots, terms):
    dma = pltpu.SemaphoreType.DMA
    return [
        pltpu.VMEM((2 * width // TILE * SHARED, FINE, TILE), BF16),
        pltpu.VMEM((SLICES, ZONES * slots + 1, FINE, TILE), BF16),
        pltpu.VMEM((summed // TILE, rows, TILE), BF16),
        pltpu.VMEM((terms * TILE, TILE), BF16),
        dma((summed // TILE,)),
        dma((SLICES, width // TILE)),
        dma((SLICES, width // TILE)),
        dma((8, 2)),
        dma((8, 2)),
        dma((5, 4, 2)),
        dma((5, 4, 2)),
        dma((6, 4, 2)),
        dma((6, 4, 2)),
    ]


def fused_kernel(slots, early, terms, count, lists, row_there, col_there, blocks, amplitudes, out, ladder, *scratch):
    swap = scratch[:count]
    meanwhile = functools.partial(one_hots, row_there, col_there, *swap[-7:-4])
    ladder_steps(slots, early, terms, lists, blocks, amplitudes, ladder, meanwhile, *scratch[count:])
    exchange_steps(ladder, out, *swap)


def packed(form, lists, amplitudes, integrals, row_mirror, col_mirror):
    slots, early, terms = FORMS[form]
    (rows, summed), width = amplitudes.shape, integrals.shape[1]
    swap = exchange_scratch(rows, width)
    return pl.pallas_call(
        functools.partial(fused_kernel, slots, early, terms, len(swap)),
        out_shape=jax.ShapeDtypeStruct((rows, width), F32),
        in_specs=[pl.BlockSpec(memory_space=pltpu.SMEM)] + [VMEM] * 3 + [pl.BlockSpec(memory_space=pl.ANY)],
        out_specs=VMEM,
        scratch_shapes=[pltpu.VMEM((rows, width), F32)] + swap + ladder_scratch(rows, summed, width, slots, terms),
        compiler_params=pltpu.CompilerParams(
            collective_id=2 + form, has_side_effects=True, vmem_limit_bytes=56 << 20
        ),
        name="packed",
    )(
        lists,
        *mirror_tables(row_mirror, col_mirror),
        integrals.reshape(integrals.shape[0] // TILE, SLICES, FINE, width),
        amplitudes,
    )


def lists_kernel(irrep, spin, lists, chosen):
    vir, occ, _, _ = place()
    across = irrep[...] * SPINS + spin[...]
    down = upright(across)
    tiles = down.shape[0]
    number = lax.broadcasted_iota(jnp.int32, (tiles, tiles), 0)
    other = lax.broadcasted_iota(jnp.int32, (tiles, tiles), 1)
    equal = down == across
    one = jnp.where(equal, 1, 0)
    prior = jnp.where(other < number, one, 0)
    total = functools.partial(jnp.sum, keepdims=True, dtype=jnp.int32)
    rank = total(prior, axis=1)
    zone_rank = total(jnp.where(other // SHARED == number // SHARED, prior, 0), axis=1)
    before = (number < other) & (number // 8 == other // 8)
    slot = zone_rank + jnp.zeros((tiles, tiles), jnp.int32)
    widest = jnp.zeros((1, 1), jnp.int32)
    for zone in range(ZONES):
        members = total(jnp.where(other // SHARED == zone, one, 0), axis=1)
        start = total(jnp.where(before, members, 0), axis=0)
        slot += jnp.where(number // SHARED == zone, start, 0)
        group = total(jnp.where(number // 8 == other // 8, members, 0), axis=0)
        widest = jnp.maximum(widest, jnp.max(group, axis=1, keepdims=True))
    longest = jnp.max(total(one, axis=0), axis=1, keepdims=True)
    form = jnp.full((1, 1), len(FORMS), jnp.int32)
    stride = jnp.zeros((1, 1), jnp.int32)
    for f, (slots, _, terms) in reversed(list(enumerate(FORMS))):
        fits = (widest <= slots) & (longest <= terms)
        form = jnp.where(fits, f, form)
        stride = jnp.where(fits, slots, stride)

    entry = lax.broadcasted_iota(jnp.int32, (tiles, TILE), 1)
    tile = lax.broadcasted_iota(jnp.int32, (tiles, TILE), 0)

    filled = jnp.where(equal, slot + 1, 0)

    def column(a):
        return total(jnp.where(other == a, filled, 0), axis=1)

    pack = jnp.zeros((1, TILE), jnp.int32)
    here = tile // SHARED == occ // 4
    for a in range(8):
        hit = here & (column(vir // 2 * 8 + a) == entry + 1)
        pack += total(jnp.where(hit, a * SHARED + tile % SHARED, 0), axis=0)
    lists[0:1, :] = pack
    for t in range(4):
        place_plus = column(vir * 4 + t)
        hit = (place_plus > 0) & (rank == entry)
        at = tile // SHARED * stride + place_plus - 1 - ZONES * stride
        lists[1 + t : 2 + t, :] = ZONES * stride + total(jnp.where(hit, at, 0), axis=0)
        lists[5 + t : 6 + t, :] = total(jnp.where(hit, tile, 0), axis=0)
    chosen[0, 0] = jnp.max(form)


def tile_lists(tile_irrep, tile_spin):
    return pl.pallas_call(
        lists_kernel,
        out_shape=(jax.ShapeDtypeStruct((16, TILE), jnp.int32), jax.ShapeDtypeStruct((1, 1), jnp.int32)),
        in_specs=[VMEM] * 2,
        out_specs=(VMEM, pl.BlockSpec(memory_space=pltpu.SMEM)),
        name="lists",
    )(tile_irrep[None, :], tile_spin[None, :])


def full_ladder(amplitudes, integrals, code):
    row_count, col_count = integrals.shape
    row_tiles = row_count // TILE
    col_tiles = col_count // TILE
    row_codes = lax.dynamic_slice_in_dim(code, lax.axis_index("occ") * row_tiles, row_tiles)
    col_codes = lax.dynamic_slice_in_dim(code, lax.axis_index("vir") * col_tiles, col_tiles)
    allowed = row_codes[:, None] == col_codes[None, :]
    masked = jnp.where(
        allowed[:, None, :, None], integrals.reshape(row_tiles, TILE, col_tiles, TILE), 0
    ).reshape(row_count, col_count)
    return jnp.dot(amplitudes, lax.all_gather(masked, "occ", axis=0, tiled=True), preferred_element_type=F32)


def local(amplitudes, integrals, tile_irrep, tile_spin, row_mirror, col_mirror, occ_gap, vir_energy):
    lists, chosen = tile_lists(tile_irrep, tile_spin)

    def whole():
        ladder = full_ladder(amplitudes, integrals, tile_irrep * SPINS + tile_spin)
        return exchanged(ladder, row_mirror, col_mirror)

    forms = [
        functools.partial(packed, form, lists, amplitudes, integrals, row_mirror, col_mirror)
        for form in range(len(FORMS))
    ]
    residual = lax.switch(chosen[0, 0], forms + [whole])
    return residual / (occ_gap[:, None] + vir_energy[None, :])


def solution(mesh):
    placed = (P("occ", None), P("occ", "vir"), P(), P(), P("occ"), P("vir"), P("occ"), P("vir"))
    return jax.shard_map(local, mesh=mesh, in_specs=placed, out_specs=P("occ", "vir"), check_vma=False)
```
